32 devices in a mesh: groups: 2 (over y), block: 4 (over z), rep: 2 (over x), tile: 2 (over core).
Axes of the slice: x: 2, y: 2, z: 4, core: 2. Of those that a mesh axis runs over, the one named last changes fastest.
Arguments:
- visible: int32 [8, 512, 2], P(('groups', 'block'), ('rep', 'tile')), parts along dimension 0, may hold values from 0 to 11, all different within a row; in each aligned block of 128 rows (0 to 127, 128 to 255, ..., all dimensions but the last counted through in order) at most 43 rows name the same one
- bins: int32 [8, 512, 2, 16], P(('groups', 'block'), ('rep', 'tile')), parts along dimension 0, may hold values from 0 to 255, as said below
- ray_code: bfloat16 [8, 512, 128], P(('groups', 'block'), ('rep', 'tile')), parts along dimension 0, may hold values from -6 to 6
- blend: float32 [8, 512, 2], P(('groups', 'block'), ('rep', 'tile')), parts along dimension 0, may hold values from 0.2 to 5
- truth: float32 [3, 8, 512], P(None, ('groups', 'block'), ('rep', 'tile')), parts along dimension 1, may hold values from 0 to 1
- w_in: bfloat16 [12, 144, 512], P('block'), may hold values from -0.75 to 0.75
- w_hid: bfloat16 [12, 512, 512], P('block'), may hold values from -0.375 to 0.375
- w_out: bfloat16 [12, 4, 512], P('block'), may hold values from -0.5 to 0.5
Outputs:
- rendered: float32 [3, 8, 512], P(None, ('groups', 'block'), ('rep', 'tile')), parts along dimension 1
- flip_map: float32 [8, 512], P(('groups', 'block'), ('rep', 'tile')), parts along dimension 0
- psnr: float32 [2], P('groups'), parts along dimension 0
The draws below stay inside these ranges and needn't reach their ends.
There are 2 independent parts, one for each index of `groups`. The reference program is written for one: setup_inputs(seed, part) draws one part's arguments, and reference() takes and returns one part's arrays. A program takes and returns all parts, laid end to end along the dimension named above; an argument that names none is the same for every part. Nothing has to cross between parts.
Inputs may be any that keep to these rules, and one draw needn't show every extreme that they name: `visible`: each pixel names 2 different blocks; among the 128 pixels of one device no block is named by more than 43 pixels, and some block is named by exactly 43. `bins`: sample j of every list lies in [j * 16, (j + 1) * 16), so each list rises.
All inputs are finite; a program needn't handle non-finite values.
Results may differ from the reference program's by a relative error of at most 0.00061.
Values may be sent and summed in bfloat16 or wider, within the bound.
No kernel may reach another device: no remote copies, remote signals or barrier semaphores. Data moves between devices by JAX's collectives and lax.ppermute only.
A program may use at most 64 MiB of HBM per device.

```python
import math
import jax
import jax.numpy as jnp
import numpy as np
from jax import lax

D = 512
RC = 128
DC = 16
IN = 144
NBINS = 256
S = 16
TW = 128
VIS = 2
BLOCKS = 12
CAP = 43
H = 4
W = 512
N_BLOCK = 4
N_REP = 2
N_TILE = 2


def draw_bins(key, part):
    key = jax.random.fold_in(key, 3)
    stride = NBINS // S
    offset = jax.random.randint(key, (H, W, VIS, S), 0, stride, dtype=jnp.int32)
    return offset + stride * jnp.arange(S, dtype=jnp.int32)


def draw_truth(key, part):
    key = jax.random.fold_in(key, 7)
    row_ramp = jnp.arange(H, dtype=jnp.float32)[:, None] / max(H - 1, 1)
    column_ramp = jnp.arange(W, dtype=jnp.float32)[None, :] / max(W - 1, 1)
    amplitude = 0.045 * jnp.power(10.0, 0.5 * (row_ramp + column_ramp))
    jitter = jax.random.uniform(key, (3, H, W), jnp.float32, -1.0, 1.0)
    return 0.5 + amplitude * jitter


def block_scale(key, extent, cuts, low, largest):
    def one(position, blocks):
        heights = jax.random.uniform(jax.random.fold_in(jax.random.fold_in(key, 6), position), (blocks,), jnp.float32, low / len(cuts), largest / len(cuts))
        return jnp.repeat(jnp.exp(heights), extent[position] // blocks).reshape((-1,) + (1,) * (len(extent) - position - 1))

    factor_of = one(*cuts[0])
    for cut in cuts[1:]:
        factor_of = factor_of * one(*cut)
    return factor_of


def shared_out(stream_key, own, number, rows, amount, top, bound, slope):
    sequence = jax.random.permutation(stream_key, amount)
    crowded, common = portions_of(amount, rows * top, bound, slope, True), portions_of(amount, rows * top, bound, slope, False)
    places = jnp.arange(amount)

    def named(lengths, offset_by):
        used = int((lengths > 0).sum())
        fixed = max(1, used // 4)
        moved = fixed + (places - fixed + offset_by * (used - fixed)) % max(1, amount - fixed)
        return jnp.zeros((amount,), jnp.int32).at[sequence[jnp.where(places < fixed, places, moved)]].set(jnp.asarray(lengths, jnp.int32))

    lengths = jnp.where(number % 4 == 0, named(crowded, number // 4), named(common, number - number // 4 - 1))
    mixed = jax.random.permutation(jax.random.fold_in(own, 3), amount)
    source_of, sink = mixed[0:amount // 2 * 2:2], mixed[1:amount // 2 * 2:2]
    room = jnp.minimum(lengths[source_of] - 1, bound - lengths[sink]) // 2
    room = jnp.where((source_of == sequence[0]) | (sink == sequence[0]) | (lengths[sink] == 0), 0, jnp.maximum(room, 0))
    moved = jax.random.randint(jax.random.fold_in(own, 4), (amount // 2,), 0, 1 << 20) % (room + 1)
    lengths = lengths.at[source_of].add(-moved).at[sink].add(moved)
    labels = jnp.searchsorted(jnp.cumsum(lengths), jnp.arange(rows * top), side="right").astype(jnp.int32)
    listing = labels.reshape(top, rows).T
    listing = listing[jax.random.permutation(jax.random.fold_in(own, 1), rows)]
    offset_by = jax.random.randint(jax.random.fold_in(own, 2), (rows, 1), 0, top)
    return jnp.take_along_axis(listing, (jnp.arange(top)[None, :] + offset_by) % top, axis=1)


def portions_of(count, total, bound, slope, full):
    portions = [(1 << 20) // math.isqrt(standing ** slope) + 1 for standing in range(1, count + 1)]
    largest = bound if full else min(bound, max(-(-total // count), total * portions[0] // sum(portions)))
    least = 1 if total - largest >= count - 1 else 0
    counts, rest = [largest] + [least] * (count - 1), total - largest - least * (count - 1)
    while rest > 0:
        candidates = [i for i in range(1, count) if counts[i] < largest] or [i for i in range(1, count) if counts[i] < bound]
        mass, left = sum([portions[i] for i in candidates]), rest
        for i in candidates:
            more = min(bound - counts[i], max(1, left * portions[i] // mass), rest)
            counts[i] = counts[i] + more
            rest = rest - more
    return np.array(counts)


def noise(rng, shape, width, reach, cuts=(), kind=jnp.bfloat16):
    drawn = width * jax.random.normal(rng, shape, jnp.float32)
    if cuts:
        drawn = drawn * block_scale(rng, shape, cuts, -0.22, 0.18)
    return jnp.clip(drawn, -reach, reach).astype(kind)


def setup_inputs(seed: int = 0, part: int = 0) -> dict:
    seeds = jax.random.split(jax.random.key(seed), 9)
    own_keys = jax.random.split(jax.random.fold_in(seeds[8], part), 9)
    visible_keys = jax.random.split(jax.random.fold_in(own_keys[0], 1), H * W // TW)
    visible_turns = jax.random.permutation(jax.random.fold_in(own_keys[0], 3), H * W // TW)
    visible = jax.vmap(lambda own, number: shared_out(jax.random.fold_in(own_keys[0], 2), own, number, TW, BLOCKS, VIS, CAP, 2))(visible_keys, visible_turns).reshape((H, W, VIS))
    bins = draw_bins(jax.random.fold_in(jax.random.fold_in(seeds[8], part), 71), part)
    ray_code = noise(own_keys[2], (H, W, RC), 1.0, 6.0, ((0, 4), (1, 4)))
    blend = jnp.clip(jnp.exp(math.log(5.0) - 3.218876 * jax.random.uniform(own_keys[3], (H, W, VIS), jnp.float32) ** block_scale(own_keys[3], (H, W, VIS), ((0, 4), (1, 4)), -0.2, 0.2)), 0.2, 5.0)
    truth = draw_truth(jax.random.fold_in(jax.random.fold_in(seeds[8], part), 71), part)
    w_in = noise(seeds[5], (BLOCKS, IN, D), (IN // 2) ** -0.5, 0.75, ((0, 4),))
    w_hid = noise(seeds[6], (BLOCKS, D, D), (D // 2) ** -0.5, 0.375, ((0, 4),))
    w_out = noise(seeds[7], (BLOCKS, 4, D), (D // 4) ** -0.5, 0.5, ((0, 4),))
    return {"visible": visible, "bins": bins, "ray_code": ray_code, "blend": blend, "truth": truth, "w_in": w_in, "w_hid": w_hid, "w_out": w_out}


OPPONENT = ((0.2126, 0.7152, 0.0722), (0.5, -0.5, 0.0), (0.0, 0.4, -0.4))
SPREAD = (0.6, 0.35, 0.35)
EMPHASIS = (1.0, 2.0, 2.0)

def make_inputs(ray_codes, depth_bins):
    pair_num = depth_bins.shape[0]
    sample_num = depth_bins.shape[1]
    powers = jnp.arange(DC // 2, dtype=jnp.float32)
    angles = depth_bins[:, :, None] * (jnp.pi * jnp.exp2(powers) / NBINS)
    depth_code = jnp.concatenate([jnp.sin(angles), jnp.cos(angles)], axis=2).astype(jnp.bfloat16)
    spread_codes = jnp.broadcast_to(ray_codes[:, None, :], (pair_num, sample_num, ray_codes.shape[1]))
    return jnp.concatenate([spread_codes, depth_code], axis=2)

def network(inputs, weight_in, weight_hidden, weight_out):
    pair_num = inputs.shape[0]
    sample_num = inputs.shape[1]
    flattened = inputs.reshape(pair_num * sample_num, inputs.shape[2])
    layer_one = jnp.maximum(jnp.dot(flattened, weight_in, preferred_element_type=jnp.float32), 0.0).astype(jnp.bfloat16)
    layer_two = jnp.maximum(jnp.dot(layer_one, weight_hidden, preferred_element_type=jnp.float32), 0.0).astype(jnp.bfloat16)
    outputs = lax.dot_general(weight_out, layer_two, (((1,), (1,)), ((), ())), preferred_element_type=jnp.float32)
    return outputs.reshape(4, pair_num, sample_num)

def composite(outputs):
    sample_num = outputs.shape[2]
    optical = jax.nn.softplus(outputs[0]) * (1.5 / sample_num)
    before = jnp.cumsum(optical, axis=1) - optical
    weights = jnp.exp(-before) * (1.0 - jnp.exp(-optical))
    colors = lax.optimization_barrier(jnp.sum(weights[None] * jax.nn.sigmoid(outputs[1:]), axis=2))
    return jnp.concatenate([colors, lax.optimization_barrier(jnp.sum(weights, axis=1))[None]], axis=0)

def opponent_error(rendered, truth):
    matrix = jnp.array(OPPONENT, dtype=jnp.float32)
    return jnp.einsum('ij,jhw->ihw', matrix, rendered - truth, precision=lax.Precision.HIGHEST)

def flip_from(padded):
    neighbour = jnp.array(SPREAD, dtype=jnp.float32)[:, None, None]
    emphasis = jnp.array(EMPHASIS, dtype=jnp.float32)[:, None, None]
    rowwise = neighbour * padded[:, :-2, :] + padded[:, 1:-1, :] + neighbour * padded[:, 2:, :]
    colwise = neighbour * rowwise[:, :, :-2] + rowwise[:, :, 1:-1] + neighbour * rowwise[:, :, 2:]
    filtered = colwise / ((1.0 + 2.0 * neighbour) * (1.0 + 2.0 * neighbour))
    return jnp.sqrt(lax.optimization_barrier(jnp.sum((emphasis * filtered) ** 2, axis=0)) + 1e-06)

def reference(visible, bins, ray_code, blend, truth, w_in, w_hid, w_out):
    height = visible.shape[0]
    columns_all = visible.shape[1]
    visible_num = visible.shape[2]
    pair_total = height * columns_all * visible_num
    block_of = visible.reshape(pair_total)
    depth_all = bins.reshape(pair_total, S).astype(jnp.float32)
    codes_all = jnp.repeat(ray_code.reshape(height * columns_all, RC), visible_num, axis=0)
    row_bound = min(N_BLOCK * N_REP * N_TILE * CAP, pair_total)

    def one_block(block_idx):
        chosen = jnp.argsort((block_of != block_idx).astype(jnp.int32), stable=True)[:row_bound].astype(jnp.int32)
        inputs = make_inputs(codes_all[chosen], depth_all[chosen])
        shaded = composite(network(inputs, w_in[block_idx], w_hid[block_idx], w_out[block_idx]))
        target = jnp.where(block_of[chosen] == block_idx, chosen, pair_total).astype(jnp.int32)
        return (target, shaded.T)
    targets, shaded_all = lax.map(one_block, jnp.arange(BLOCKS, dtype=jnp.int32))
    pair_colors = jnp.zeros((pair_total, 4), jnp.float32).at[targets.reshape(-1)].set(shaded_all.reshape(-1, 4), mode='drop')
    pieces = pair_colors.reshape(height, columns_all, visible_num, 4)
    with_background = pieces[..., :3] + (1.0 - pieces[..., 3:])
    weights = blend[..., None]
    rendered = (lax.optimization_barrier(jnp.sum(weights * with_background, axis=2)) / lax.optimization_barrier(jnp.sum(weights, axis=2))).transpose(2, 0, 1)
    difference = rendered - truth
    mean_square = jnp.sum(difference * difference) / (3 * height * columns_all)
    psnr = (-10.0 * jnp.log10(mean_square + 1e-06)).reshape(1)
    padded = jnp.pad(opponent_error(rendered, truth), ((0, 0), (1, 1), (1, 1)))
    flip_map = flip_from(padded)
    return (rendered, flip_map, psnr)
```

```python
import functools
import math

import jax
import jax.numpy as jnp
import ml_dtypes
import numpy as np
from jax import lax
from jax.experimental import pallas as pl
from jax.experimental.pallas import tpu as pltpu
from jax.sharding import PartitionSpec as P

RC = 128
DC = 16
NBINS = 256
TILE = 32
EXTRA = 32

OPPONENT = ((0.2126, 0.7152, 0.0722), (0.5, -0.5, 0.0), (0.0, 0.4, -0.4))
SPREAD = (0.6, 0.35, 0.35)
EMPHASIS = (1.0, 2.0, 2.0)

F32 = jnp.float32
BF16 = jnp.bfloat16
VMEM_LIMIT = 48 * 1024 * 1024


def iota(shape, dim):
    return lax.broadcasted_iota(jnp.int32, shape, dim)


def parts_of(values):
    high = values.astype(BF16).astype(F32)
    rest = values - high
    middle = rest.astype(BF16).astype(F32)
    return [high, middle, rest - middle]


def depth_table(sample_num):
    powers = np.arange(DC // 2, dtype=np.float32)
    steps = (np.float32(np.pi) * np.exp2(powers) / np.float32(NBINS)).astype(np.float32)
    angles = np.arange(NBINS, dtype=np.float32)[:, None] * steps
    wide = angles.astype(np.float64)
    code = np.concatenate([np.sin(wide), np.cos(wide)], axis=1).astype(np.float32)
    stride = NBINS // sample_num
    table = np.zeros((NBINS, sample_num, DC), np.float32)
    for row in range(NBINS):
        table[row, row // stride] = code[row]
    return table.reshape(NBINS, sample_num * DC).astype(ml_dtypes.bfloat16)


def pack_kernel(visible, bins, ray_code, blend, truth, message):
    pixels = ray_code.shape[0]
    message[0:pixels] = ray_code[...]
    lists = bins.shape[0] * bins.shape[1]
    message[pixels : pixels + lists] = bins[...].astype(F32).reshape(lists, pixels).astype(BF16)
    truths = truth[...].reshape(truth.shape[0], pixels)
    rows = [visible[...].astype(F32)] + parts_of(blend[...]) + parts_of(truths)
    used = sum(row.shape[0] for row in rows)
    rows.append(jnp.zeros((EXTRA - used, pixels), F32))
    message[pixels + lists :] = jnp.concatenate(rows, axis=0).astype(BF16)


def serve_kernel(sources, slots, *refs):
    messages = refs[:sources]
    w_in, w_hid, w_out, table, partial, aside = refs[sources : sources + 6]
    places, mixed, codes, depths, first_w, last_w, heads = refs[sources + 6 :]
    local_blocks, in_width, hidden = w_in.shape
    pixels = messages[0].shape[1]
    lists = messages[0].shape[0] - pixels - EXTRA
    samples = lists // 2
    first_block = lax.axis_index("block") * local_blocks

    extras = [messages[s][pixels + lists :].astype(F32) for s in range(sources)]

    named = []
    for s in range(sources):
        for v in range(2):
            own = iota((8, pixels), 0) + first_block
            hit = (extras[s][v : v + 1] == own.astype(F32)) & (iota((8, pixels), 0) < local_blocks)
            named.append(hit.astype(F32))
    either = [named[2 * s] + named[2 * s + 1] for s in range(sources)]
    before = (iota((pixels, pixels), 0) < iota((pixels, pixels), 1)).astype(F32).astype(BF16)
    ranks = jnp.dot(
        jnp.concatenate(either, axis=0).astype(BF16), before, preferred_element_type=F32
    )
    offset = jnp.zeros((8, 1), F32)
    slot_row = iota((slots, pixels), 0).astype(F32)
    for s in range(sources):
        rank = ranks[8 * s : 8 * s + 8] + offset
        offset = offset + jnp.sum(either[s], axis=1, keepdims=True)
        for v in range(2):
            spot = jnp.where(named[2 * s + v] > 0.0, rank, -1.0)
            lanes = pl.ds((2 * s + v) * pixels, pixels)
            for k in range(local_blocks):
                places[k * slots : (k + 1) * slots, lanes] = (
                    (slot_row == spot[k : k + 1]).astype(F32).astype(BF16)
                )
    tiles = [
        (jnp.max(offset[k : k + 1]).astype(jnp.int32) + TILE - 1) // TILE
        for k in range(local_blocks)
    ]

    lane = iota((pixels, pixels), 1)
    per_turn = pixels // lists
    for turn in range(0, sources, per_turn):
        group = [
            messages[s][pixels : pixels + lists].astype(F32)
            for s in range(turn, min(turn + per_turn, sources))
        ]
        if len(group) < per_turn:
            group.append(jnp.zeros(((per_turn - len(group)) * lists, pixels), F32))
        turned = jnp.concatenate(group, axis=0).T
        for s in range(turn, min(turn + per_turn, sources)):
            for v in range(2):
                rows = pl.ds((2 * s + v) * pixels, pixels)
                mine = lane // samples == 2 * (s - turn) + v
                mixed[rows, 0:RC] = messages[s][0:pixels]
                mixed[rows, RC:] = jnp.where(mine, turned, 0.0).astype(BF16)

    chosen = jnp.dot(places[...], mixed[...], preferred_element_type=F32).astype(BF16)
    codes[...] = chosen[:, :RC]
    spread_shape = (pixels, samples * DC)
    spread = (iota(spread_shape, 0) % samples == iota(spread_shape, 1) // DC).astype(F32)
    bins = jnp.dot(chosen[:, RC:], spread.astype(BF16), preferred_element_type=F32)
    is_bin = (bins == iota(bins.shape, 1).astype(F32)).astype(F32).astype(BF16)
    depths[...] = jnp.dot(is_bin, table[...], preferred_element_type=F32).astype(BF16)

    heads[...] = jnp.zeros_like(heads)
    per_half = RC // DC
    for k in range(local_blocks):
        first_w[0:RC] = w_in[k, 0:RC]
        for i in range(per_half):
            first_w[RC + i * DC : RC + (i + 1) * DC] = w_in[k, RC:]
        wide = jnp.concatenate(
            [jnp.broadcast_to(w_out[k, c : c + 1].astype(F32), (samples, hidden)) for c in range(4)]
            + [jnp.zeros((128 - 4 * samples, hidden), F32)],
            axis=0,
        )
        last_w[...] = wide.T.astype(BF16)

        def one_tile(t, carry, k=k):
            rows = pl.ds(pl.multiple_of(k * slots + t * TILE, TILE), TILE)
            code = codes[rows, :]
            depth = depths[rows, :]
            half_lane = iota((TILE, RC), 1) // DC
            inputs = []
            for j in range(samples):
                half = depth[:, (j // per_half) * RC : (j // per_half + 1) * RC]
                kept = jnp.where(half_lane == j % per_half, half, jnp.zeros_like(half))
                inputs.append(jnp.concatenate([code, kept], axis=1))
            inputs = jnp.concatenate(inputs, axis=0)
            one = jnp.dot(inputs, first_w[...], preferred_element_type=F32)
            one = jnp.maximum(one, 0.0).astype(BF16)
            two = jnp.dot(one, w_hid[k], preferred_element_type=F32)
            two = jnp.maximum(two, 0.0).astype(BF16)
            out = jnp.dot(two, last_w[...], preferred_element_type=F32)
            sample_lane = iota((TILE, 128), 1) % samples
            total = jnp.zeros((TILE, 128), F32)
            for j in range(samples):
                total = jnp.where(sample_lane == j, out[j * TILE : (j + 1) * TILE], total)
            heads[rows, :] = total
            return carry

        lax.fori_loop(0, tiles[k], one_tile, 0)

    turned = heads[...].T
    optical = jax.nn.softplus(turned[0:samples]) * (1.5 / samples)
    lower = (iota((samples, samples), 1) < iota((samples, samples), 0)).astype(F32)
    ahead = jnp.dot(
        jnp.concatenate([lower] * 3, axis=1).astype(BF16),
        jnp.concatenate(parts_of(optical), axis=0).astype(BF16),
        preferred_element_type=F32,
    )
    weights = jnp.exp(-ahead) * (1.0 - jnp.exp(-optical))
    background = 1.0 - jnp.sum(weights, axis=0, keepdims=True)
    shades = []
    for c in range(1, 4):
        color = jax.nn.sigmoid(turned[c * samples : (c + 1) * samples])
        shades.append(jnp.sum(weights * color, axis=0, keepdims=True) + background)
    shades.append(jnp.zeros_like(background))
    shades = jnp.concatenate(shades, axis=0)[:, : local_blocks * slots]
    stacked = jnp.concatenate(parts_of(shades) + [jnp.zeros_like(shades)], axis=0).astype(BF16)
    spots = jnp.dot(stacked, places[...], preferred_element_type=F32)
    spots = spots[0:4] + spots[4:8] + spots[8:12]
    for s in range(sources):
        blend = [extras[s][2 + v : 3 + v] + extras[s][4 + v : 5 + v] + extras[s][6 + v : 7 + v] for v in range(2)]
        lanes = slice(s * pixels, (s + 1) * pixels)
        mine = [spots[:, (2 * s + v) * pixels : (2 * s + v + 1) * pixels] * blend[v] for v in range(2)]
        partial[:, lanes] = mine[0] + mine[1]
        aside[0:3, lanes] = extras[s][8:11] + extras[s][11:14] + extras[s][14:17]
        aside[3:4, lanes] = blend[0] + blend[1]


def gather_kernel(sources, *refs):
    partials = refs[:sources]
    aside, rendered, message = refs[sources:]
    pixels = rendered.shape[2]
    z = lax.axis_index("block")

    def block(ref, u):
        return ref[:, u * pixels : (u + 1) * pixels]

    squared = jnp.zeros((3, pixels), F32)
    rows = []
    for u in range(sources):
        total = block(partials[0], u)
        for t in range(1, sources):
            total = total + block(partials[t], t ^ u)
        extra = block(aside, u)
        shown = total[0:3] / extra[3:4]
        if u == 0:
            rendered[...] = shown.reshape(3, 1, pixels)
        difference = shown - extra[0:3]
        squared = squared + difference * difference
        rows.append(difference)
    above = jnp.zeros((3, pixels), F32)
    below = jnp.zeros((3, pixels), F32)
    for u in range(1, sources):
        above = above + jnp.where((z ^ u) == z - 1, rows[u], 0.0)
        below = below + jnp.where((z ^ u) == z + 1, rows[u], 0.0)
    for c in range(3):
        def channel(d):
            return sum(OPPONENT[c][i] * d[i : i + 1] for i in range(3) if OPPONENT[c][i])

        message[c : c + 1] = SPREAD[c] * channel(above) + channel(rows[0]) + SPREAD[c] * channel(below)
    total = jnp.sum(jnp.sum(squared, axis=0, keepdims=True), axis=1, keepdims=True)
    message[3:4] = jnp.broadcast_to(total, (1, pixels))


def finish_kernel(columns, count, *refs):
    messages = refs[:columns]
    flip_map, psnr = refs[columns:]
    pixels = flip_map.shape[1]
    q = lax.axis_index("rep") * lax.axis_size("tile") + lax.axis_index("tile")
    own = messages[0][...]
    left = jnp.zeros_like(own)
    right = jnp.zeros_like(own)
    total = own[3:4]
    for s in range(1, columns):
        other = messages[s][...]
        left = left + jnp.where((q ^ s) == q - 1, other, 0.0)
        right = right + jnp.where((q ^ s) == q + 1, other, 0.0)
        total = total + other[3:4]
    lane = iota(own.shape, 1)
    before = pltpu.roll(jnp.where(lane == pixels - 1, left, own), 1, 1)
    after = pltpu.roll(jnp.where(lane == 0, right, own), pixels - 1, 1)
    summed = jnp.zeros((1, pixels), F32)
    for c in range(3):
        column = SPREAD[c] * before[c : c + 1] + own[c : c + 1] + SPREAD[c] * after[c : c + 1]
        scale = np.float32(1.0) + np.float32(2.0) * np.float32(SPREAD[c])
        filtered = column / float(scale * scale)
        emphasised = EMPHASIS[c] * filtered
        summed = summed + emphasised * emphasised
    flip_map[...] = jnp.sqrt(summed + 1e-06)
    logged = jnp.log(total / count + 1e-06) * (-10.0 / math.log(10.0))
    psnr[...] = logged[:, 0:1]


def exchange(value, axes, size):
    out = [value]
    for s in range(1, size):
        out.append(lax.ppermute(value, axes, [(i, i ^ s) for i in range(size)]))
    return out


def call(kernel, out_shape, scratch=(), flops=0, bytes_accessed=0):
    return pl.pallas_call(
        kernel,
        out_shape=out_shape,
        scratch_shapes=list(scratch),
        compiler_params=pltpu.CompilerParams(vmem_limit_bytes=VMEM_LIMIT),
    )


def body(visible, bins, ray_code, blend, truth, w_in, w_hid, w_out):
    sources = lax.axis_size("block")
    columns = lax.axis_size("rep") * lax.axis_size("tile")
    local_blocks, in_width, hidden = w_in.shape
    pixels = visible.shape[1]
    visible_num = visible.shape[2]
    samples = bins.shape[3]
    blocks_all = local_blocks * sources
    capacity = (2 * pixels * visible_num + blocks_all - 1) // blocks_all
    slots = -(-sources * capacity // TILE) * TILE
    slots_all = local_blocks * slots
    lists = visible_num * samples
    height = pixels + lists + EXTRA

    message = call(pack_kernel, jax.ShapeDtypeStruct((height, pixels), BF16))(
        visible.reshape(pixels, visible_num).T,
        jnp.transpose(bins.reshape(pixels, visible_num, samples), (1, 2, 0)),
        ray_code.reshape(pixels, RC),
        blend.reshape(pixels, visible_num).T,
        truth,
    )
    messages = exchange(message, "block", sources)
    partial, aside = call(
        functools.partial(serve_kernel, sources, slots),
        (
            jax.ShapeDtypeStruct((4, sources * pixels), F32),
            jax.ShapeDtypeStruct((4, sources * pixels), F32),
        ),
        (
            pltpu.VMEM((slots_all, sources * visible_num * pixels), BF16),
            pltpu.VMEM((sources * visible_num * pixels, 2 * RC), BF16),
            pltpu.VMEM((slots_all, RC), BF16),
            pltpu.VMEM((slots_all, samples * DC), BF16),
            pltpu.VMEM((2 * RC, hidden), BF16),
            pltpu.VMEM((hidden, 128), BF16),
            pltpu.VMEM((-(-slots_all // 128) * 128, 128), F32),
        ),
    )(*messages, w_in, w_hid, w_out, jnp.asarray(depth_table(samples)))
    partials = exchange(partial, "block", sources)
    rendered, edge = call(
        functools.partial(gather_kernel, sources),
        (
            jax.ShapeDtypeStruct((3, 1, pixels), F32),
            jax.ShapeDtypeStruct((4, pixels), F32),
        ),
    )(*partials, aside)
    edges = exchange(edge, ("rep", "tile"), columns)
    flip_map, psnr = call(
        functools.partial(finish_kernel, columns, 3 * sources * columns * pixels),
        (
            jax.ShapeDtypeStruct((1, pixels), F32),
            jax.ShapeDtypeStruct((1, 1), F32),
        ),
    )(*edges)
    return (rendered, flip_map, psnr.reshape(1))


def solution(mesh):
    placed = (
        P(("groups", "block"), ("rep", "tile"), None),
        P(("groups", "block"), ("rep", "tile"), None, None),
        P(("groups", "block"), ("rep", "tile"), None),
        P(("groups", "block"), ("rep", "tile"), None),
        P(None, ("groups", "block"), ("rep", "tile")),
        P("block", None, None),
        P("block", None, None),
        P("block", None, None),
    )
    return jax.shard_map(
        body,
        mesh=mesh,
        in_specs=placed,
        out_specs=(
            P(None, ("groups", "block"), ("rep", "tile")),
            P(("groups", "block"), ("rep", "tile")),
            P("groups"),
        ),
        check_vma=False,
    )
```

```python
import functools
import math

import jax
import jax.numpy as jnp
import ml_dtypes
import numpy as np
from jax import lax
from jax.experimental import pallas as pl
from jax.experimental.pallas import tpu as pltpu
from jax.sharding import PartitionSpec as P

RC = 128
DC = 16
NBINS = 256
EXTRA = 16

OPPONENT = ((0.2126, 0.7152, 0.0722), (0.5, -0.5, 0.0), (0.0, 0.4, -0.4))
SPREAD = (0.6, 0.35, 0.35)
EMPHASIS = (1.0, 2.0, 2.0)

F32 = jnp.float32
BF16 = jnp.bfloat16


def iota(shape, dim):
    return lax.broadcasted_iota(jnp.int32, shape, dim)


def parts_of(values):
    high = values.astype(BF16).astype(F32)
    rest = values - high
    middle = rest.astype(BF16).astype(F32)
    return [high, middle, rest - middle]


def depth_table(sample_num):
    powers = np.arange(DC // 2, dtype=np.float32)
    steps = (np.float32(np.pi) * np.exp2(powers) / np.float32(NBINS)).astype(np.float32)
    angles = np.arange(NBINS, dtype=np.float32)[:, None] * steps
    wide = angles.astype(np.float64)
    code = np.concatenate([np.sin(wide), np.cos(wide)], axis=1).astype(np.float32)
    stride = NBINS // sample_num
    table = np.zeros((NBINS, sample_num, DC), np.float32)
    for row in range(NBINS):
        table[row, row // stride] = code[row]
    return table.reshape(NBINS, sample_num * DC).astype(ml_dtypes.bfloat16)


def pack_kernel(visible, bins, ray_code, blend, truth, message, names, lists, weights, truths, sems):
    pixels = ray_code.shape[0]
    listed = bins.shape[0] * bins.shape[1]
    copies = [
        pltpu.make_async_copy(source, target, sems.at[i])
        for i, (source, target) in enumerate(
            (
                (ray_code, message.at[0:pixels]),
                (bins, lists),
                (visible, names),
                (blend, weights),
                (truth, truths),
            )
        )
    ]
    for copy in copies:
        copy.start()
    for copy in copies[1:]:
        copy.wait()
    message[pixels : pixels + listed] = lists[...].astype(F32).reshape(listed, pixels).astype(BF16)
    shares = weights[...] / jnp.sum(weights[...], axis=0, keepdims=True)
    rows = [names[...].astype(F32)] + parts_of(shares)
    used = sum(row.shape[0] for row in rows)
    rows.append(jnp.zeros((EXTRA - used, pixels), F32))
    message[pixels + listed :] = jnp.concatenate(rows, axis=0).astype(BF16)
    copies[0].wait()


def tiles_for(most, large, small):
    tiles = []
    start = 0
    while start < most:
        for size in small + [large]:
            low = small[small.index(size) - 1] if size in small[1:] else 0
            if size == large:
                low = small[-1]
            if low < most - start:
                high = start + size if size != large else most
                tiles.append((start, size, start + low, high))
        start += large
    return tiles


def prepare_kernel(samples, w_in, w_hid, w_out, first_w, hid_w, last_w, sem):
    local_blocks, in_width, hidden = w_in.shape
    load = pltpu.make_async_copy(w_hid, hid_w, sem)
    load.start()
    for k in range(local_blocks):
        first_w[k, 0:RC] = w_in[k, 0:RC]
        for i in range(RC // DC):
            first_w[k, RC + i * DC : RC + (i + 1) * DC] = w_in[k, RC:]
        wide = jnp.concatenate(
            [
                jnp.broadcast_to(w_out[k, c : c + 1].astype(F32), (samples, hidden))
                for c in range(4)
            ]
            + [jnp.zeros((128 - 4 * samples, hidden), F32)],
            axis=0,
        )
        last_w[k] = wide.T.astype(BF16)
    load.wait()


def serve_kernel(sources, slots, tiles, *refs):
    messages = refs[:sources]
    truth, first_w, w_hid, last_w, table, partial = refs[sources : sources + 6]
    places, mixed, codes, depths, heads = refs[sources + 6 :]
    local_blocks = w_hid.shape[0]
    pixels = messages[0].shape[1]
    lists = messages[0].shape[0] - pixels - EXTRA
    samples = lists // 2
    first_block = lax.axis_index("block") * local_blocks

    extras = [messages[s][pixels + lists :].astype(F32) for s in range(sources)]

    named = []
    for s in range(sources):
        for v in range(2):
            block = iota((8, pixels), 0) + first_block
            hit = (extras[s][v : v + 1] == block.astype(F32)) & (
                iota((8, pixels), 0) < local_blocks
            )
            named.append(hit.astype(F32))
    either = [named[2 * s] + named[2 * s + 1] for s in range(sources)]
    before = (iota((pixels, pixels), 0) < iota((pixels, pixels), 1)).astype(F32).astype(BF16)
    ranks = jnp.dot(
        jnp.concatenate(either, axis=0).astype(BF16), before, preferred_element_type=F32
    )
    offset = jnp.zeros((8, 1), F32)
    slot_row = iota((slots, pixels), 0).astype(F32)
    for s in range(sources):
        rank = ranks[8 * s : 8 * s + 8] + offset
        offset = offset + jnp.sum(either[s], axis=1, keepdims=True)
        for v in range(2):
            spot = jnp.where(named[2 * s + v] > 0.0, rank, -1.0)
            lanes = pl.ds((2 * s + v) * pixels, pixels)
            for k in range(local_blocks):
                places[k * slots : (k + 1) * slots, lanes] = (
                    (slot_row == spot[k : k + 1]).astype(F32).astype(BF16)
                )
    counts = [jnp.max(offset[k : k + 1]).astype(jnp.int32) for k in range(local_blocks)]

    lane = iota((pixels, pixels), 1)
    per_turn = pixels // lists
    for turn in range(0, sources, per_turn):
        group = [
            messages[s][pixels : pixels + lists].astype(F32)
            for s in range(turn, min(turn + per_turn, sources))
        ]
        if len(group) < per_turn:
            group.append(jnp.zeros(((per_turn - len(group)) * lists, pixels), F32))
        turned = jnp.concatenate(group, axis=0).T
        for s in range(turn, min(turn + per_turn, sources)):
            for v in range(2):
                rows = pl.ds((2 * s + v) * pixels, pixels)
                mine = lane // samples == 2 * (s - turn) + v
                mixed[rows, 0:RC] = messages[s][0:pixels]
                mixed[rows, RC:] = jnp.where(mine, turned, 0.0).astype(BF16)

    chosen = jnp.dot(places[...], mixed[...], preferred_element_type=F32).astype(BF16)
    codes[...] = chosen[:, :RC]
    spread_shape = (pixels, samples * DC)
    spread = (iota(spread_shape, 0) % samples == iota(spread_shape, 1) // DC).astype(F32)
    bins = jnp.dot(chosen[:, RC:], spread.astype(BF16), preferred_element_type=F32)
    is_bin = (bins == iota(bins.shape, 1).astype(F32)).astype(F32).astype(BF16)
    depths[...] = jnp.dot(is_bin, table[...], preferred_element_type=F32).astype(BF16)

    heads[...] = jnp.zeros_like(heads)
    per_half = RC // DC
    for k in range(local_blocks):

        def one_tile(start, size, k=k):
            rows = pl.ds(pl.multiple_of(k * slots + start, 16), size)
            code = codes[rows, :]
            depth = depths[rows, :]
            half_lane = iota((size, RC), 1) // DC
            inputs = []
            for j in range(samples):
                half = depth[:, (j // per_half) * RC : (j // per_half + 1) * RC]
                kept = jnp.where(half_lane == j % per_half, half, jnp.zeros_like(half))
                inputs.append(jnp.concatenate([code, kept], axis=1))
            inputs = jnp.concatenate(inputs, axis=0)
            one = jnp.dot(inputs, first_w[k], preferred_element_type=F32)
            one = jnp.maximum(one, 0.0).astype(BF16)
            two = jnp.dot(one, w_hid[k], preferred_element_type=F32)
            two = jnp.maximum(two, 0.0).astype(BF16)
            out = jnp.dot(two, last_w[k], preferred_element_type=F32)
            sample_lane = iota((size, 128), 1) % samples
            total = jnp.zeros((size, 128), F32)
            for j in range(samples):
                total = jnp.where(sample_lane == j, out[j * size : (j + 1) * size], total)
            heads[rows, :] = total

        for start, size, fewest, most in tiles:

            @pl.when((counts[k] > fewest) & (counts[k] <= most))
            def _(one_tile=one_tile, start=start, size=size):
                one_tile(start, size)

    turned = heads[...].T
    optical = jax.nn.softplus(turned[0:samples]) * (1.5 / samples)
    lower = (iota((samples, samples), 1) < iota((samples, samples), 0)).astype(F32)
    ahead = jnp.dot(
        jnp.concatenate([lower] * 3, axis=1).astype(BF16),
        jnp.concatenate(parts_of(optical), axis=0).astype(BF16),
        preferred_element_type=F32,
    )
    weights = jnp.exp(-ahead) * (1.0 - jnp.exp(-optical))
    background = 1.0 - jnp.sum(weights, axis=0, keepdims=True)
    shades = []
    for c in range(1, 4):
        color = jax.nn.sigmoid(turned[c * samples : (c + 1) * samples])
        shades.append(jnp.sum(weights * color, axis=0, keepdims=True) + background)
    shades.append(jnp.zeros_like(background))
    shades = jnp.concatenate(shades, axis=0)[:, : local_blocks * slots]
    stacked = jnp.concatenate(parts_of(shades) + [jnp.zeros_like(shades)], axis=0).astype(BF16)
    spots = jnp.dot(stacked, places[...], preferred_element_type=F32)
    spots = spots[0:4] + spots[4:8] + spots[8:12]
    sums = []
    for s in range(sources):
        mine = []
        for v in range(2):
            share = extras[s][2 + v : 3 + v] + extras[s][4 + v : 5 + v] + extras[s][6 + v : 7 + v]
            mine.append(spots[0:3, (2 * s + v) * pixels : (2 * s + v + 1) * pixels] * share)
        sums.append(mine[0] + mine[1])
    sums[0] = sums[0] - truth[...].reshape(3, pixels)
    partial[...] = jnp.concatenate(sums, axis=0)


def gather_kernel(sources, *refs):
    partials = refs[:sources]
    truth, rendered, message = refs[sources:]
    pixels = rendered.shape[2]
    z = lax.axis_index("block")
    squared = jnp.zeros((3, pixels), F32)
    rows = []
    for u in range(sources):
        difference = partials[0][3 * u : 3 * u + 3]
        for t in range(1, sources):
            difference = difference + partials[t][3 * (t ^ u) : 3 * (t ^ u) + 3]
        if u == 0:
            rendered[...] = difference.reshape(3, 1, pixels) + truth[...]
        squared = squared + difference * difference
        rows.append(difference)
    above = jnp.zeros((3, pixels), F32)
    below = jnp.zeros((3, pixels), F32)
    for u in range(1, sources):
        above = above + jnp.where((z ^ u) == z - 1, rows[u], 0.0)
        below = below + jnp.where((z ^ u) == z + 1, rows[u], 0.0)

    def opponent(block, c):
        return sum(OPPONENT[c][i] * block[i : i + 1] for i in range(3) if OPPONENT[c][i])

    mixed = [
        SPREAD[c] * opponent(above, c) + opponent(rows[0], c) + SPREAD[c] * opponent(below, c)
        for c in range(3)
    ]
    total = jnp.sum(jnp.sum(squared, axis=0, keepdims=True), axis=1, keepdims=True)
    message[...] = jnp.concatenate(mixed + [jnp.broadcast_to(total, (1, pixels))], axis=0)


def finish_kernel(columns, count, *refs):
    messages = refs[:columns]
    flip_map, psnr = refs[columns:]
    pixels = flip_map.shape[1]
    q = lax.axis_index("rep") * lax.axis_size("tile") + lax.axis_index("tile")
    own = messages[0][...]
    left = jnp.zeros_like(own)
    right = jnp.zeros_like(own)
    total = own[3:4]
    for s in range(1, columns):
        other = messages[s][...]
        left = left + jnp.where((q ^ s) == q - 1, other, 0.0)
        right = right + jnp.where((q ^ s) == q + 1, other, 0.0)
        total = total + other[3:4]
    lane = iota(own.shape, 1)
    before = pltpu.roll(jnp.where(lane == pixels - 1, left, own), 1, 1)
    after = pltpu.roll(jnp.where(lane == 0, right, own), pixels - 1, 1)
    summed = jnp.zeros((1, pixels), F32)
    for c in range(3):
        column = SPREAD[c] * before[c : c + 1] + own[c : c + 1] + SPREAD[c] * after[c : c + 1]
        scale = np.float32(1.0) + np.float32(2.0) * np.float32(SPREAD[c])
        emphasised = EMPHASIS[c] * (column / float(scale * scale))
        summed = summed + emphasised * emphasised
    flip_map[...] = jnp.sqrt(summed + 1e-06)
    logged = jnp.log(total / count + 1e-06) * (-10.0 / math.log(10.0))
    psnr[...] = logged[:, 0:1]


def exchange(value, axes, size):
    out = [value]
    for s in range(1, size):
        out.append(lax.ppermute(value, axes, [(i, i ^ s) for i in range(size)]))
    return out


def call(
    kernel, out_shape, in_specs, scratch, flops=0, bytes_accessed=0, limit=8 << 20
):
    cost = None
    if flops:
        cost = pl.CostEstimate(flops=flops, bytes_accessed=bytes_accessed, transcendentals=0)
    return pl.pallas_call(
        kernel,
        out_shape=out_shape,
        in_specs=in_specs,
        scratch_shapes=list(scratch),
        cost_estimate=cost,
        compiler_params=pltpu.CompilerParams(vmem_limit_bytes=limit),
    )


def body(visible, bins, ray_code, blend, truth, w_in, w_hid, w_out):
    sources = lax.axis_size("block")
    columns = lax.axis_size("rep") * lax.axis_size("tile")
    local_blocks, in_width, hidden = w_in.shape
    pixels = visible.shape[1]
    visible_num = visible.shape[2]
    samples = bins.shape[3]
    blocks_all = local_blocks * sources
    capacity = (2 * pixels * visible_num + blocks_all - 1) // blocks_all
    lists = visible_num * samples
    height = pixels + lists + EXTRA
    far = pl.BlockSpec(memory_space=pltpu.HBM)
    near = pl.BlockSpec(memory_space=pltpu.VMEM)
    message = call(
        pack_kernel,
        jax.ShapeDtypeStruct((height, pixels), BF16),
        [far] * 5,
        (
            pltpu.VMEM((visible_num, pixels), jnp.int32),
            pltpu.VMEM((visible_num, samples, pixels), jnp.int32),
            pltpu.VMEM((visible_num, pixels), F32),
            pltpu.VMEM(truth.shape, F32),
            pltpu.SemaphoreType.DMA((5,)),
        ),
        limit=64 << 20,
    )(
        visible.reshape(pixels, visible_num).T,
        jnp.transpose(bins.reshape(pixels, visible_num, samples), (1, 2, 0)),
        ray_code.reshape(pixels, RC),
        blend.reshape(pixels, visible_num).T,
        truth,
    )
    messages = exchange(message, "block", sources)
    table = jnp.asarray(depth_table(samples))

    slots = -(-sources * capacity // 16) * 16
    tiles = tiles_for(slots, 96, [48, 80])
    slots_all = local_blocks * slots
    first_w, hid_w, last_w = call(
        functools.partial(prepare_kernel, samples),
        (
            jax.ShapeDtypeStruct((local_blocks, 2 * RC, hidden), BF16),
            jax.ShapeDtypeStruct(w_hid.shape, BF16),
            jax.ShapeDtypeStruct((local_blocks, hidden, 128), BF16),
        ),
        [near, far, near],
        (pltpu.SemaphoreType.DMA,),
        limit=8 * 1024 * 1024,
        flops=1 << 20,
        bytes_accessed=1 << 22,
    )(w_in, w_hid, w_out)
    partial = call(
        functools.partial(serve_kernel, sources, slots, tiles),
        jax.ShapeDtypeStruct((3 * sources, pixels), F32),
        [near] * (sources + 5),
        (
            pltpu.VMEM((slots_all, sources * visible_num * pixels), BF16),
            pltpu.VMEM((sources * visible_num * pixels, 2 * RC), BF16),
            pltpu.VMEM((slots_all, RC), BF16),
            pltpu.VMEM((slots_all, samples * DC), BF16),
            pltpu.VMEM((-(-slots_all // 128) * 128, 128), F32),
        ),
        flops=2 * slots_all * samples * hidden * (in_width + hidden + 4),
        bytes_accessed=2 * (w_in.size + w_hid.size),
        limit=40 * 1024 * 1024,
    )(*messages, truth, first_w, hid_w, last_w, table)
    partials = exchange(partial, "block", sources)
    rendered, edge = call(
        functools.partial(gather_kernel, sources),
        (
            jax.ShapeDtypeStruct((3, 1, pixels), F32),
            jax.ShapeDtypeStruct((4, pixels), F32),
        ),
        [near] * (sources + 1),
        (),
    )(*partials, truth)
    edges = exchange(edge, ("rep", "tile"), columns)
    flip_map, psnr = call(
        functools.partial(finish_kernel, columns, 3 * sources * columns * pixels),
        (
            jax.ShapeDtypeStruct((1, pixels), F32),
            jax.ShapeDtypeStruct((1, 1), F32),
        ),
        [near] * columns,
        (),
    )(*edges)
    return (rendered, flip_map, psnr.reshape(1))


def solution(mesh):
    placed = (
        P(("groups", "block"), ("rep", "tile"), None),
        P(("groups", "block"), ("rep", "tile"), None, None),
        P(("groups", "block"), ("rep", "tile"), None),
        P(("groups", "block"), ("rep", "tile"), None),
        P(None, ("groups", "block"), ("rep", "tile")),
        P("block", None, None),
        P("block", None, None),
        P("block", None, None),
    )
    return jax.shard_map(
        body,
        mesh=mesh,
        in_specs=placed,
        out_specs=(
            P(None, ("groups", "block"), ("rep", "tile")),
            P(("groups", "block"), ("rep", "tile")),
            P("groups"),
        ),
        check_vma=False,
    )
```

```python
import functools
import math

import jax
import jax.numpy as jnp
import ml_dtypes
import numpy as np
from jax import lax
from jax.experimental import pallas as pl
from jax.experimental.pallas import tpu as pltpu
from jax.sharding import PartitionSpec as P

RC = 128
DC = 16
NBINS = 256
EXTRA = 16

OPPONENT = ((0.2126, 0.7152, 0.0722), (0.5, -0.5, 0.0), (0.0, 0.4, -0.4))
SPREAD = (0.6, 0.35, 0.35)
EMPHASIS = (1.0, 2.0, 2.0)

F32 = jnp.float32
BF16 = jnp.bfloat16


def iota(shape, dim):
    return lax.broadcasted_iota(jnp.int32, shape, dim)


def parts_of(values):
    high = values.astype(BF16).astype(F32)
    rest = values - high
    middle = rest.astype(BF16).astype(F32)
    return [high, middle, rest - middle]


def depth_table(sample_num):
    powers = np.arange(DC // 2, dtype=np.float32)
    steps = (np.float32(np.pi) * np.exp2(powers) / np.float32(NBINS)).astype(np.float32)
    angles = np.arange(NBINS, dtype=np.float32)[:, None] * steps
    wide = angles.astype(np.float64)
    code = np.concatenate([np.sin(wide), np.cos(wide)], axis=1).astype(np.float32)
    stride = NBINS // sample_num
    table = np.zeros((NBINS, sample_num, DC), np.float32)
    for row in range(NBINS):
        table[row, row // stride] = code[row]
    return table.reshape(NBINS, sample_num * DC).astype(ml_dtypes.bfloat16)


def blank_kernel(rows):
    rows[...] = jnp.zeros_like(rows)


def pack_kernel(visible, bins, ray_code, blend, blank, message):
    pixels = ray_code.shape[0]
    listed = bins.shape[0] * bins.shape[1]
    message[0:pixels] = ray_code[...]
    message[pixels : pixels + listed] = bins[...].astype(F32).reshape(listed, pixels).astype(BF16)
    shares = blend[...] / jnp.sum(blend[...], axis=0, keepdims=True)
    rows = [visible[...].astype(F32)] + parts_of(shares) + [blank[...]]
    message[pixels + listed :] = jnp.concatenate(rows, axis=0).astype(BF16)


def tiles_for(most, sizes):
    bounds = [0] + [size for size in sizes if size < most] + [most]
    return [(high, low, high) for low, high in zip(bounds, bounds[1:])]


def layout_kernel(samples, before, spread):
    before[...] = (iota(before.shape, 0) < iota(before.shape, 1)).astype(F32).astype(BF16)
    here = iota(spread.shape, 0) % samples == iota(spread.shape, 1) // DC
    spread[...] = here.astype(F32).astype(BF16)


def prepare_kernel(samples, w_in, w_hid, w_out, first_w, hid_w, last_w, sem):
    local_blocks, in_width, hidden = w_in.shape
    load = pltpu.make_async_copy(w_hid, hid_w, sem)
    load.start()
    for k in range(local_blocks):
        first_w[k, 0:RC] = w_in[k, 0:RC]
        for i in range(RC // DC):
            first_w[k, RC + i * DC : RC + (i + 1) * DC] = w_in[k, RC:]
        wide = jnp.concatenate(
            [
                jnp.broadcast_to(w_out[k, c : c + 1].astype(F32), (samples, hidden))
                for c in range(4)
            ]
            + [jnp.zeros((128 - 4 * samples, hidden), F32)],
            axis=0,
        )
        last_w[k] = wide.T.astype(BF16)
    load.wait()


def serve_kernel(sources, slots, tiles, *refs):
    messages = refs[:sources]
    truth, first_w, w_hid, last_w, table, before, spread, partial = refs[sources : sources + 8]
    places, mixed, codes, depths, heads = refs[sources + 8 :]
    local_blocks = w_hid.shape[0]
    pixels = messages[0].shape[1]
    lists = messages[0].shape[0] - pixels - EXTRA
    samples = lists // 2
    first_block = lax.axis_index("block") * local_blocks

    extras = [messages[s][pixels + lists :].astype(F32) for s in range(sources)]

    named = []
    for s in range(sources):
        for v in range(2):
            block = iota((8, pixels), 0) + first_block
            hit = (extras[s][v : v + 1] == block.astype(F32)) & (
                iota((8, pixels), 0) < local_blocks
            )
            named.append(hit.astype(F32))
    either = [named[2 * s] + named[2 * s + 1] for s in range(sources)]
    ranks = jnp.dot(
        jnp.concatenate(either, axis=0).astype(BF16), before[...], preferred_element_type=F32
    )
    offset = jnp.zeros((8, 1), F32)
    slot_row = iota((slots, pixels), 0).astype(F32)
    for s in range(sources):
        rank = ranks[8 * s : 8 * s + 8] + offset
        offset = offset + jnp.sum(either[s], axis=1, keepdims=True)
        for v in range(2):
            spot = jnp.where(named[2 * s + v] > 0.0, rank, -1.0)
            lanes = pl.ds((2 * s + v) * pixels, pixels)
            for k in range(local_blocks):
                places[k * slots : (k + 1) * slots, lanes] = (
                    (slot_row == spot[k : k + 1]).astype(F32).astype(BF16)
                )
    counts = [jnp.max(offset[k : k + 1]).astype(jnp.int32) for k in range(local_blocks)]

    lane = iota((pixels, pixels), 1)
    per_turn = pixels // lists
    for turn in range(0, sources, per_turn):
        group = [
            messages[s][pixels : pixels + lists].astype(F32)
            for s in range(turn, min(turn + per_turn, sources))
        ]
        if len(group) < per_turn:
            group.append(jnp.zeros(((per_turn - len(group)) * lists, pixels), F32))
        turned = jnp.concatenate(group, axis=0).T
        for s in range(turn, min(turn + per_turn, sources)):
            for v in range(2):
                rows = pl.ds((2 * s + v) * pixels, pixels)
                mine = lane // samples == 2 * (s - turn) + v
                mixed[rows, 0:RC] = messages[s][0:pixels]
                mixed[rows, RC:] = jnp.where(mine, turned, 0.0).astype(BF16)

    chosen = jnp.dot(places[...], mixed[...], preferred_element_type=F32).astype(BF16)
    codes[...] = chosen[:, :RC]
    bins = jnp.dot(chosen[:, RC:], spread[...], preferred_element_type=F32)
    is_bin = (bins == iota(bins.shape, 1).astype(F32)).astype(F32).astype(BF16)
    depths[...] = jnp.dot(is_bin, table[...], preferred_element_type=F32).astype(BF16)

    heads[...] = jnp.zeros_like(heads)
    per_half = RC // DC
    def one_block(k, carry):
        count = carry[0]
        for i in range(1, local_blocks):
            count = jnp.where(k == i, carry[i], count)

        def one_tile(start, size):
            rows = pl.ds(pl.multiple_of(k * slots + start, 16), size)
            code = codes[rows, :]
            depth = depths[rows, :]
            half_lane = iota((size, RC), 1) // DC
            inputs = []
            for j in range(samples):
                half = depth[:, (j // per_half) * RC : (j // per_half + 1) * RC]
                kept = jnp.where(half_lane == j % per_half, half, jnp.zeros_like(half))
                inputs.append(jnp.concatenate([code, kept], axis=1))
            inputs = jnp.concatenate(inputs, axis=0)
            one = jnp.dot(inputs, first_w[k], preferred_element_type=F32)
            one = jnp.maximum(one, 0.0).astype(BF16)
            two = jnp.dot(one, w_hid[k], preferred_element_type=F32)
            two = jnp.maximum(two, 0.0).astype(BF16)
            out = jnp.dot(two, last_w[k], preferred_element_type=F32)
            sample_lane = iota((size, 128), 1) % samples
            total = jnp.zeros((size, 128), F32)
            for j in range(samples):
                total = jnp.where(sample_lane == j, out[j * size : (j + 1) * size], total)
            heads[rows, :] = total

        for size, fewest, most in tiles:

            @pl.when((count > fewest) & (count <= most))
            def _(size=size):
                one_tile(0, size)

        return carry

    lax.fori_loop(0, local_blocks, one_block, tuple(counts))

    turned = heads[...].T
    optical = jax.nn.softplus(turned[0:samples]) * (1.5 / samples)
    lower = (iota((samples, samples), 1) < iota((samples, samples), 0)).astype(F32)
    ahead = jnp.dot(
        jnp.concatenate([lower] * 3, axis=1).astype(BF16),
        jnp.concatenate(parts_of(optical), axis=0).astype(BF16),
        preferred_element_type=F32,
    )
    weights = jnp.exp(-ahead) * (1.0 - jnp.exp(-optical))
    background = 1.0 - jnp.sum(weights, axis=0, keepdims=True)
    shades = []
    for c in range(1, 4):
        color = jax.nn.sigmoid(turned[c * samples : (c + 1) * samples])
        shades.append(jnp.sum(weights * color, axis=0, keepdims=True) + background)
    shades.append(jnp.zeros_like(background))
    shades = jnp.concatenate(shades, axis=0)[:, : local_blocks * slots]
    stacked = jnp.concatenate(parts_of(shades) + [jnp.zeros_like(shades)], axis=0).astype(BF16)
    spots = jnp.dot(stacked, places[...], preferred_element_type=F32)
    spots = spots[0:4] + spots[4:8] + spots[8:12]
    sums = []
    for s in range(sources):
        mine = []
        for v in range(2):
            share = extras[s][2 + v : 3 + v] + extras[s][4 + v : 5 + v] + extras[s][6 + v : 7 + v]
            mine.append(spots[0:3, (2 * s + v) * pixels : (2 * s + v + 1) * pixels] * share)
        sums.append(mine[0] + mine[1])
    sums[0] = sums[0] - truth[...].reshape(3, pixels)
    partial[...] = jnp.concatenate(sums, axis=0)


def gather_kernel(sources, *refs):
    partials = refs[:sources]
    (message,) = refs[sources:]
    pixels = message.shape[1]
    z = lax.axis_index("block")
    squared = jnp.zeros((3, pixels), F32)
    rows = []
    for u in range(sources):
        difference = partials[0][3 * u : 3 * u + 3]
        for t in range(1, sources):
            difference = difference + partials[t][3 * (t ^ u) : 3 * (t ^ u) + 3]
        squared = squared + difference * difference
        rows.append(difference)
    above = jnp.zeros((3, pixels), F32)
    below = jnp.zeros((3, pixels), F32)
    for u in range(1, sources):
        above = above + jnp.where((z ^ u) == z - 1, rows[u], 0.0)
        below = below + jnp.where((z ^ u) == z + 1, rows[u], 0.0)

    def opponent(block, c):
        return sum(OPPONENT[c][i] * block[i : i + 1] for i in range(3) if OPPONENT[c][i])

    mixed = [
        SPREAD[c] * opponent(above, c) + opponent(rows[0], c) + SPREAD[c] * opponent(below, c)
        for c in range(3)
    ]
    total = jnp.sum(jnp.sum(squared, axis=0, keepdims=True), axis=1, keepdims=True)
    message[...] = jnp.concatenate(
        mixed + [jnp.broadcast_to(total, (1, pixels)), rows[0]], axis=0
    )


def finish_kernel(columns, count, *refs):
    messages = refs[:columns]
    truth, rendered, flip_map, psnr = refs[columns:]
    pixels = flip_map.shape[1]
    q = lax.axis_index("rep") * lax.axis_size("tile") + lax.axis_index("tile")
    rendered[...] = messages[0][4:7].reshape(3, 1, pixels) + truth[...]
    own = messages[0][0:4]
    left = jnp.zeros_like(own)
    right = jnp.zeros_like(own)
    total = own[3:4]
    for s in range(1, columns):
        other = messages[s][0:4]
        left = left + jnp.where((q ^ s) == q - 1, other, 0.0)
        right = right + jnp.where((q ^ s) == q + 1, other, 0.0)
        total = total + other[3:4]
    lane = iota(own.shape, 1)
    before = pltpu.roll(jnp.where(lane == pixels - 1, left, own), 1, 1)
    after = pltpu.roll(jnp.where(lane == 0, right, own), pixels - 1, 1)
    summed = jnp.zeros((1, pixels), F32)
    for c in range(3):
        column = SPREAD[c] * before[c : c + 1] + own[c : c + 1] + SPREAD[c] * after[c : c + 1]
        scale = np.float32(1.0) + np.float32(2.0) * np.float32(SPREAD[c])
        emphasised = EMPHASIS[c] * (column / float(scale * scale))
        summed = summed + emphasised * emphasised
    flip_map[...] = jnp.sqrt(summed + 1e-06)
    logged = jnp.log(total / count + 1e-06) * (-10.0 / math.log(10.0))
    psnr[...] = logged[:, 0:1]


def exchange(value, axes, size):
    out = [value]
    for s in range(1, size):
        out.append(lax.ppermute(value, axes, [(i, i ^ s) for i in range(size)]))
    return out


def call(
    kernel, out_shape, in_specs, scratch, flops=0, bytes_accessed=0, limit=8 << 20
):
    cost = None
    if flops:
        cost = pl.CostEstimate(flops=flops, bytes_accessed=bytes_accessed, transcendentals=0)
    return pl.pallas_call(
        kernel,
        out_shape=out_shape,
        in_specs=in_specs,
        scratch_shapes=list(scratch),
        cost_estimate=cost,
        compiler_params=pltpu.CompilerParams(vmem_limit_bytes=limit),
    )


def body(visible, bins, ray_code, blend, truth, w_in, w_hid, w_out):
    sources = lax.axis_size("block")
    columns = lax.axis_size("rep") * lax.axis_size("tile")
    local_blocks, in_width, hidden = w_in.shape
    pixels = visible.shape[1]
    visible_num = visible.shape[2]
    samples = bins.shape[3]
    blocks_all = local_blocks * sources
    capacity = (2 * pixels * visible_num + blocks_all - 1) // blocks_all
    lists = visible_num * samples
    height = pixels + lists + EXTRA
    far = pl.BlockSpec(memory_space=pltpu.HBM)
    near = pl.BlockSpec(memory_space=pltpu.VMEM)
    blank = call(
        blank_kernel,
        jax.ShapeDtypeStruct((EXTRA - 4 * visible_num, pixels), F32),
        [],
        (),
        flops=1 << 32,
        bytes_accessed=1 << 17,
    )()
    message = call(
        pack_kernel, jax.ShapeDtypeStruct((height, pixels), BF16), [near] * 5, ()
    )(
        visible.reshape(pixels, visible_num).T,
        jnp.transpose(bins.reshape(pixels, visible_num, samples), (1, 2, 0)),
        ray_code.reshape(pixels, RC),
        blend.reshape(pixels, visible_num).T,
        blank,
    )
    messages = exchange(message, "block", sources)
    table = jnp.asarray(depth_table(samples))

    slots = -(-sources * capacity // 16) * 16
    tiles = tiles_for(slots, list(range(16, slots, 16)))
    slots_all = local_blocks * slots
    before, spread = call(
        functools.partial(layout_kernel, samples),
        (
            jax.ShapeDtypeStruct((pixels, pixels), BF16),
            jax.ShapeDtypeStruct((pixels, samples * DC), BF16),
        ),
        [],
        (),
        limit=8 * 1024 * 1024,
        flops=1 << 32,
        bytes_accessed=1 << 17,
    )()
    first_w, hid_w, last_w = call(
        functools.partial(prepare_kernel, samples),
        (
            jax.ShapeDtypeStruct((local_blocks, 2 * RC, hidden), BF16),
            jax.ShapeDtypeStruct(w_hid.shape, BF16),
            jax.ShapeDtypeStruct((local_blocks, hidden, 128), BF16),
        ),
        [near, far, near],
        (pltpu.SemaphoreType.DMA,),
        limit=8 * 1024 * 1024,
        flops=1 << 20,
        bytes_accessed=1 << 22,
    )(w_in, w_hid, w_out)
    partial = call(
        functools.partial(serve_kernel, sources, slots, tiles),
        jax.ShapeDtypeStruct((3 * sources, pixels), F32),
        [near] * (sources + 7),
        (
            pltpu.VMEM((slots_all, sources * visible_num * pixels), BF16),
            pltpu.VMEM((sources * visible_num * pixels, 2 * RC), BF16),
            pltpu.VMEM((slots_all, RC), BF16),
            pltpu.VMEM((slots_all, samples * DC), BF16),
            pltpu.VMEM((-(-slots_all // 128) * 128, 128), F32),
        ),
        flops=2 * slots_all * samples * hidden * (in_width + hidden + 4),
        bytes_accessed=2 * (w_in.size + w_hid.size),
        limit=40 * 1024 * 1024,
    )(*messages, truth, first_w, hid_w, last_w, table, before, spread)
    partials = exchange(partial, "block", sources)
    edge = call(
        functools.partial(gather_kernel, sources),
        jax.ShapeDtypeStruct((7, pixels), F32),
        [near] * sources,
        (),
    )(*partials)
    edges = exchange(edge, ("rep", "tile"), columns)
    rendered, flip_map, psnr = call(
        functools.partial(finish_kernel, columns, 3 * sources * columns * pixels),
        (
            jax.ShapeDtypeStruct((3, 1, pixels), F32),
            jax.ShapeDtypeStruct((1, pixels), F32),
            jax.ShapeDtypeStruct((1, 1), F32),
        ),
        [near] * (columns + 1),
        (),
    )(*edges, truth)
    return (rendered, flip_map, psnr.reshape(1))


def solution(mesh):
    placed = (
        P(("groups", "block"), ("rep", "tile"), None),
        P(("groups", "block"), ("rep", "tile"), None, None),
        P(("groups", "block"), ("rep", "tile"), None),
        P(("groups", "block"), ("rep", "tile"), None),
        P(None, ("groups", "block"), ("rep", "tile")),
        P("block", None, None),
        P("block", None, None),
        P("block", None, None),
    )
    return jax.shard_map(
        body,
        mesh=mesh,
        in_specs=placed,
        out_specs=(
            P(None, ("groups", "block"), ("rep", "tile")),
            P(("groups", "block"), ("rep", "tile")),
            P("groups"),
        ),
        check_vma=False,
    )
```

```python
import functools
import math

import jax
import jax.numpy as jnp
import ml_dtypes
import numpy as np
from jax import lax
from jax.experimental import pallas as pl
from jax.experimental.pallas import tpu as pltpu
from jax.sharding import PartitionSpec as P

RC = 128
DC = 16
NBINS = 256
EXTRA = 16
LISTS = 64
SPLIT = True

OPPONENT = ((0.2126, 0.7152, 0.0722), (0.5, -0.5, 0.0), (0.0, 0.4, -0.4))
SPREAD = (0.6, 0.35, 0.35)
EMPHASIS = (1.0, 2.0, 2.0)

F32 = jnp.float32
BF16 = jnp.bfloat16


def iota(shape, dim):
    return lax.broadcasted_iota(jnp.int32, shape, dim)


def parts_of(values):
    high = values.astype(BF16).astype(F32)
    rest = values - high
    middle = rest.astype(BF16).astype(F32)
    return [high, middle, rest - middle]


def depth_table(sample_num):
    powers = np.arange(DC // 2, dtype=np.float32)
    steps = (np.float32(np.pi) * np.exp2(powers) / np.float32(NBINS)).astype(np.float32)
    angles = np.arange(NBINS, dtype=np.float32)[:, None] * steps
    wide = angles.astype(np.float64)
    code = np.concatenate([np.sin(wide), np.cos(wide)], axis=1).astype(np.float32)
    stride = NBINS // sample_num
    table = np.zeros((NBINS, sample_num, DC), np.float32)
    for row in range(NBINS):
        table[row, row // stride] = code[row]
    return table.reshape(NBINS, sample_num * DC).astype(ml_dtypes.bfloat16)


def blank_kernel(rows):
    rows[...] = jnp.zeros_like(rows)


def pack_kernel(bins, ray_code, blank, message):
    pixels = ray_code.shape[0]
    listed = bins.shape[0] * bins.shape[1]
    message[0:pixels] = ray_code[...]
    message[pixels : pixels + listed] = bins[...].astype(F32).reshape(listed, pixels).astype(BF16)
    message[pixels + listed :] = blank[...]


def tiles_for(most, sizes):
    bounds = [0] + [size for size in sizes if size < most] + [most]
    return [(high, low, high) for low, high in zip(bounds, bounds[1:])]


def layout_kernel(samples, visible, blend, lines, message, before, spread):
    before[...] = (iota(before.shape, 0) < iota(before.shape, 1)).astype(F32).astype(BF16)
    row = iota(spread.shape[1:], 0)
    here = row % samples == iota(spread.shape[1:], 1) // DC
    for k in range(spread.shape[0]):
        mine = here & (row % LISTS // samples == k)
        spread[k] = mine.astype(F32).astype(BF16)
    shares = blend[...] / jnp.sum(blend[...], axis=0, keepdims=True)
    rows = [visible[...].astype(F32)] + parts_of(shares)
    rows.append(jnp.zeros((EXTRA - 4 * visible.shape[0], visible.shape[1]), F32))
    message[message.shape[0] - EXTRA :] = jnp.concatenate(rows, axis=0).astype(BF16)


def prepare_kernel(samples, w_in, w_hid, w_out, first_w, hid_w, last_w, sem):
    local_blocks, in_width, hidden = w_in.shape
    load = pltpu.make_async_copy(w_hid, hid_w, sem)
    load.start()
    for k in range(local_blocks):
        first_w[k, 0:RC] = w_in[k, 0:RC]
        for i in range(RC // DC):
            first_w[k, RC + i * DC : RC + (i + 1) * DC] = w_in[k, RC:]
        wide = jnp.concatenate(
            [
                jnp.broadcast_to(w_out[k, c : c + 1].astype(F32), (samples, hidden))
                for c in range(4)
            ]
            + [jnp.zeros((128 - 4 * samples, hidden), F32)],
            axis=0,
        )
        last_w[k] = wide.T.astype(BF16)
    load.wait()


def serve_kernel(own, sources, slots, tiles, *refs):
    messages = refs[:sources]
    aside, first_w, w_hid, last_w, table, before, spread, partial = refs[sources : sources + 8]
    places, mixed, codes, depths, heads = refs[sources + 8 :]
    local_blocks = w_hid.shape[0]
    pixels = messages[0].shape[1]
    lists = messages[0].shape[0] - pixels - EXTRA
    samples = lists // 2
    first_block = lax.axis_index("block") * local_blocks

    extras = [messages[s][pixels + lists :].astype(F32) for s in range(sources)]

    named = []
    for s in range(sources):
        block = iota((8, pixels), 0)
        known = (block + first_block).astype(F32)
        named.append(
            [
                ((extras[s][v : v + 1] == known) & (block < local_blocks)).astype(F32)
                for v in range(2)
            ]
        )
    either = [first + second for first, second in named]
    ranks = jnp.dot(
        jnp.concatenate(either, axis=0).astype(BF16), before[...], preferred_element_type=F32
    )
    offset = jnp.zeros((8, 1), F32)
    slot_row = iota((slots, pixels), 0).astype(F32)
    for s in range(sources):
        spot = jnp.where(either[s] > 0.0, ranks[8 * s : 8 * s + 8] + offset, -1.0)
        offset = offset + jnp.sum(either[s], axis=1, keepdims=True)
        for k in range(local_blocks):
            places[k * slots : (k + 1) * slots, s * pixels : (s + 1) * pixels] = (
                (slot_row == spot[k : k + 1]).astype(F32).astype(BF16)
            )
    counts = [jnp.max(offset[k : k + 1]).astype(jnp.int32) for k in range(local_blocks)]

    lane = iota((pixels, pixels), 1)
    per_turn = pixels // LISTS
    for turn in range(0, sources, per_turn):
        group = []
        for s in range(turn, min(turn + per_turn, sources)):
            bins = messages[s][pixels : pixels + lists].astype(F32)
            for k in range(local_blocks):
                group.append(
                    jnp.where(named[s][0][k : k + 1] > 0.0, bins[:samples], bins[samples:])
                )
            group.append(jnp.zeros((LISTS - local_blocks * samples, pixels), F32))
        rows = sum(part.shape[0] for part in group)
        if rows < pixels:
            group.append(jnp.zeros((pixels - rows, pixels), F32))
        turned = jnp.concatenate(group, axis=0).T
        for s in range(turn, min(turn + per_turn, sources)):
            mixed[s * pixels : (s + 1) * pixels, 0:RC] = messages[s][0:pixels]
            mixed[s * pixels : (s + 1) * pixels, RC:] = jnp.where(
                lane // LISTS == s - turn, turned, 0.0
            ).astype(BF16)

    chosen = jnp.dot(places[...], mixed[...], preferred_element_type=F32).astype(BF16)
    codes[...] = chosen[:, :RC]
    bins = jnp.concatenate(
        [
            jnp.dot(
                chosen[k * slots : (k + 1) * slots, RC:], spread[k], preferred_element_type=F32
            )
            for k in range(local_blocks)
        ],
        axis=0,
    )
    is_bin = (bins == iota(bins.shape, 1).astype(F32)).astype(F32).astype(BF16)
    depths[...] = jnp.dot(is_bin, table[...], preferred_element_type=F32).astype(BF16)

    heads[...] = jnp.zeros_like(heads)
    per_half = RC // DC
    def one_block(k, carry):
        count = carry[0]
        for i in range(1, local_blocks):
            count = jnp.where(k == i, carry[i], count)

        def one_tile(start, size):
            rows = pl.ds(pl.multiple_of(k * slots + start, 16), size)
            code = codes[rows, :]
            depth = depths[rows, :]
            half_lane = iota((size, RC), 1) // DC
            inputs = []
            for j in range(samples):
                half = depth[:, (j // per_half) * RC : (j // per_half + 1) * RC]
                kept = jnp.where(half_lane == j % per_half, half, jnp.zeros_like(half))
                inputs.append(jnp.concatenate([code, kept], axis=1))
            inputs = jnp.concatenate(inputs, axis=0)
            one = jnp.dot(inputs, first_w[k], preferred_element_type=F32)
            one = jnp.maximum(one, 0.0).astype(BF16)
            two = jnp.dot(one, w_hid[k], preferred_element_type=F32)
            two = jnp.maximum(two, 0.0).astype(BF16)
            out = jnp.dot(two, last_w[k], preferred_element_type=F32)
            sample_lane = iota((size, 128), 1) % samples
            total = jnp.zeros((size, 128), F32)
            for j in range(samples):
                total = jnp.where(sample_lane == j, out[j * size : (j + 1) * size], total)
            heads[rows, :] = total

        for size, fewest, most in tiles:

            @pl.when((count > fewest) & (count <= most))
            def _(size=size):
                one_tile(0, size)

        return carry

    lax.fori_loop(0, local_blocks, one_block, tuple(counts))

    turned = heads[...].T
    optical = jax.nn.softplus(turned[0:samples]) * (1.5 / samples)
    lower = (iota((samples, samples), 1) < iota((samples, samples), 0)).astype(F32)
    ahead = jnp.dot(
        jnp.concatenate([lower] * 3, axis=1).astype(BF16),
        jnp.concatenate(parts_of(optical), axis=0).astype(BF16),
        preferred_element_type=F32,
    )
    weights = jnp.exp(-ahead) * (1.0 - jnp.exp(-optical))
    background = 1.0 - jnp.sum(weights, axis=0, keepdims=True)
    shades = []
    for c in range(1, 4):
        color = jax.nn.sigmoid(turned[c * samples : (c + 1) * samples])
        shades.append(jnp.sum(weights * color, axis=0, keepdims=True) + background)
    shades.append(jnp.zeros_like(background))
    shades = jnp.concatenate(shades, axis=0)[:, : local_blocks * slots]
    stacked = jnp.concatenate(parts_of(shades) + [jnp.zeros_like(shades)], axis=0).astype(BF16)
    sums = [jnp.zeros((3, pixels), F32)] * sources
    for k in range(local_blocks):
        spots = jnp.dot(
            stacked[:, k * slots : (k + 1) * slots],
            places[k * slots : (k + 1) * slots],
            preferred_element_type=F32,
        )
        spots = spots[0:4] + spots[4:8] + spots[8:12]
        for s in range(sources):
            share = jnp.zeros((1, pixels), F32)
            for v in range(2):
                part = extras[s][2 + v : 3 + v] + extras[s][4 + v : 5 + v] + extras[s][6 + v : 7 + v]
                share = share + named[s][v][k : k + 1] * part
            sums[s] = sums[s] + spots[0:3, s * pixels : (s + 1) * pixels] * share
    if own is None:
        sums[0] = sums[0] - aside[...].reshape(3, pixels)
        partial[...] = jnp.concatenate(sums, axis=0)
    elif own:
        partial[...] = sums[0] - aside[...].reshape(3, pixels)
    else:
        partial[...] = jnp.concatenate([aside[...]] + sums, axis=0)


def gather_kernel(sources, *refs):
    partials = refs[:sources]
    (message,) = refs[sources:]
    pixels = message.shape[1]
    z = lax.axis_index("block")
    squared = jnp.zeros((3, pixels), F32)
    rows = []
    for u in range(sources):
        difference = partials[0][3 * u : 3 * u + 3]
        for t in range(1, sources):
            difference = difference + partials[t][3 * (t ^ u) : 3 * (t ^ u) + 3]
        squared = squared + difference * difference
        rows.append(difference)
    above = jnp.zeros((3, pixels), F32)
    below = jnp.zeros((3, pixels), F32)
    for u in range(1, sources):
        above = above + jnp.where((z ^ u) == z - 1, rows[u], 0.0)
        below = below + jnp.where((z ^ u) == z + 1, rows[u], 0.0)

    def opponent(block, c):
        return sum(OPPONENT[c][i] * block[i : i + 1] for i in range(3) if OPPONENT[c][i])

    mixed = [
        SPREAD[c] * opponent(above, c) + opponent(rows[0], c) + SPREAD[c] * opponent(below, c)
        for c in range(3)
    ]
    total = jnp.sum(jnp.sum(squared, axis=0, keepdims=True), axis=1, keepdims=True)
    message[...] = jnp.concatenate(
        mixed + [jnp.broadcast_to(total, (1, pixels)), rows[0]], axis=0
    )


def finish_kernel(columns, count, *refs):
    messages = refs[:columns]
    truth, rendered, flip_map, psnr = refs[columns:]
    pixels = flip_map.shape[1]
    q = lax.axis_index("rep") * lax.axis_size("tile") + lax.axis_index("tile")
    rendered[...] = messages[0][4:7].reshape(3, 1, pixels) + truth[...]
    own = messages[0][0:4]
    left = jnp.zeros_like(own)
    right = jnp.zeros_like(own)
    total = own[3:4]
    for s in range(1, columns):
        other = messages[s][0:4]
        left = left + jnp.where((q ^ s) == q - 1, other, 0.0)
        right = right + jnp.where((q ^ s) == q + 1, other, 0.0)
        total = total + other[3:4]
    lane = iota(own.shape, 1)
    before = pltpu.roll(jnp.where(lane == pixels - 1, left, own), 1, 1)
    after = pltpu.roll(jnp.where(lane == 0, right, own), pixels - 1, 1)
    summed = jnp.zeros((1, pixels), F32)
    for c in range(3):
        column = SPREAD[c] * before[c : c + 1] + own[c : c + 1] + SPREAD[c] * after[c : c + 1]
        scale = np.float32(1.0) + np.float32(2.0) * np.float32(SPREAD[c])
        emphasised = EMPHASIS[c] * (column / float(scale * scale))
        summed = summed + emphasised * emphasised
    flip_map[...] = jnp.sqrt(summed + 1e-06)
    logged = jnp.log(total / count + 1e-06) * (-10.0 / math.log(10.0))
    psnr[...] = logged[:, 0:1]


def exchange(value, axes, size):
    out = [value]
    for s in range(1, size):
        out.append(lax.ppermute(value, axes, [(i, i ^ s) for i in range(size)]))
    return out


def call(
    kernel, out_shape, in_specs, scratch, flops=0, bytes_accessed=0, limit=8 << 20, aliases=None
):
    cost = None
    if flops:
        cost = pl.CostEstimate(flops=flops, bytes_accessed=bytes_accessed, transcendentals=0)
    return pl.pallas_call(
        kernel,
        out_shape=out_shape,
        in_specs=in_specs,
        scratch_shapes=list(scratch),
        cost_estimate=cost,
        input_output_aliases=aliases or {},
        compiler_params=pltpu.CompilerParams(vmem_limit_bytes=limit),
    )


def body(visible, bins, ray_code, blend, truth, w_in, w_hid, w_out):
    sources = lax.axis_size("block")
    columns = lax.axis_size("rep") * lax.axis_size("tile")
    local_blocks, in_width, hidden = w_in.shape
    pixels = visible.shape[1]
    visible_num = visible.shape[2]
    samples = bins.shape[3]
    blocks_all = local_blocks * sources
    capacity = (2 * pixels * visible_num + blocks_all - 1) // blocks_all
    lists = visible_num * samples
    height = pixels + lists + EXTRA
    far = pl.BlockSpec(memory_space=pltpu.HBM)
    near = pl.BlockSpec(memory_space=pltpu.VMEM)
    blank = call(
        blank_kernel,
        jax.ShapeDtypeStruct((EXTRA, pixels), BF16),
        [],
        (),
        flops=1 << 32,
        bytes_accessed=1 << 17,
    )()
    lines = call(
        pack_kernel, jax.ShapeDtypeStruct((height, pixels), BF16), [near] * 3, ()
    )(
        jnp.transpose(bins.reshape(pixels, visible_num, samples), (1, 2, 0)),
        ray_code.reshape(pixels, RC),
        blank,
    )
    message, before, spread = call(
        functools.partial(layout_kernel, samples),
        (
            jax.ShapeDtypeStruct((height, pixels), BF16),
            jax.ShapeDtypeStruct((pixels, pixels), BF16),
            jax.ShapeDtypeStruct((local_blocks, pixels, samples * DC), BF16),
        ),
        [near] * 3,
        (),
        flops=1 << 32,
        bytes_accessed=1 << 17,
        aliases={2: 0},
    )(visible.reshape(pixels, visible_num).T, blend.reshape(pixels, visible_num).T, lines)
    messages = exchange(message, "block", sources)
    table = jnp.asarray(depth_table(samples))

    first_w, hid_w, last_w = call(
        functools.partial(prepare_kernel, samples),
        (
            jax.ShapeDtypeStruct((local_blocks, 2 * RC, hidden), BF16),
            jax.ShapeDtypeStruct(w_hid.shape, BF16),
            jax.ShapeDtypeStruct((local_blocks, hidden, 128), BF16),
        ),
        [near, far, near],
        (pltpu.SemaphoreType.DMA,),
        limit=8 * 1024 * 1024,
        flops=1 << 20,
        bytes_accessed=1 << 22,
    )(w_in, w_hid, w_out)

    def serve(own, parts, aside):
        count = len(parts)
        slots = -(-count * capacity // 16) * 16
        slots_all = local_blocks * slots
        return call(
            functools.partial(
                serve_kernel, own, count, slots, tiles_for(slots, list(range(16, slots, 16)))
            ),
            jax.ShapeDtypeStruct((3 * count + 3 * (own is False), pixels), F32),
            [near] * (count + 7),
            (
                pltpu.VMEM((slots_all, count * pixels), BF16),
                pltpu.VMEM((count * pixels, 2 * RC), BF16),
                pltpu.VMEM((slots_all, RC), BF16),
                pltpu.VMEM((slots_all, samples * DC), BF16),
                pltpu.VMEM((-(-slots_all // 128) * 128, 128), F32),
            ),
            flops=2 * slots_all * samples * hidden * (in_width + hidden + 4),
            bytes_accessed=2 * (w_in.size + w_hid.size),
            limit=40 * 1024 * 1024,
        )(*parts, aside, first_w, hid_w, last_w, table, before, spread)

    if SPLIT:
        partial = serve(False, messages[1:], serve(True, messages[:1], truth))
    else:
        partial = serve(None, messages, truth)
    partials = exchange(partial, "block", sources)
    edge = call(
        functools.partial(gather_kernel, sources),
        jax.ShapeDtypeStruct((7, pixels), F32),
        [near] * sources,
        (),
    )(*partials)
    edges = exchange(edge, ("rep", "tile"), columns)
    rendered, flip_map, psnr = call(
        functools.partial(finish_kernel, columns, 3 * sources * columns * pixels),
        (
            jax.ShapeDtypeStruct((3, 1, pixels), F32),
            jax.ShapeDtypeStruct((1, pixels), F32),
            jax.ShapeDtypeStruct((1, 1), F32),
        ),
        [near] * (columns + 1),
        (),
    )(*edges, truth)
    return (rendered, flip_map, psnr.reshape(1))


def solution(mesh):
    placed = (
        P(("groups", "block"), ("rep", "tile"), None),
        P(("groups", "block"), ("rep", "tile"), None, None),
        P(("groups", "block"), ("rep", "tile"), None),
        P(("groups", "block"), ("rep", "tile"), None),
        P(None, ("groups", "block"), ("rep", "tile")),
        P("block", None, None),
        P("block", None, None),
        P("block", None, None),
    )
    return jax.shard_map(
        body,
        mesh=mesh,
        in_specs=placed,
        out_specs=(
            P(None, ("groups", "block"), ("rep", "tile")),
            P(("groups", "block"), ("rep", "tile")),
            P("groups"),
        ),
        check_vma=False,
    )
```

```python
import functools
import math

import jax
import jax.numpy as jnp
import ml_dtypes
import numpy as np
from jax import lax
from jax.experimental import pallas as pl
from jax.experimental.pallas import tpu as pltpu
from jax.sharding import PartitionSpec as P

RC = 128
DC = 16
NBINS = 256
EXTRA = 16
LISTS = 64

OPPONENT = ((0.2126, 0.7152, 0.0722), (0.5, -0.5, 0.0), (0.0, 0.4, -0.4))
SPREAD = (0.6, 0.35, 0.35)
EMPHASIS = (1.0, 2.0, 2.0)

F32 = jnp.float32
BF16 = jnp.bfloat16


def iota(shape, dim):
    return lax.broadcasted_iota(jnp.int32, shape, dim)


def parts_of(values):
    high = values.astype(BF16).astype(F32)
    rest = values - high
    middle = rest.astype(BF16).astype(F32)
    return [high, middle, rest - middle]


def depth_table(sample_num):
    powers = np.arange(DC // 2, dtype=np.float32)
    steps = (np.float32(np.pi) * np.exp2(powers) / np.float32(NBINS)).astype(np.float32)
    angles = np.arange(NBINS, dtype=np.float32)[:, None] * steps
    wide = angles.astype(np.float64)
    code = np.concatenate([np.sin(wide), np.cos(wide)], axis=1).astype(np.float32)
    stride = NBINS // sample_num
    table = np.zeros((NBINS, sample_num, DC), np.float32)
    for row in range(NBINS):
        table[row, row // stride] = code[row]
    return table.reshape(NBINS, sample_num * DC).astype(ml_dtypes.bfloat16)


def blank_kernel(rows):
    rows[...] = jnp.zeros_like(rows)


def pack_kernel(bins, ray_code, blank, message):
    pixels = ray_code.shape[0]
    listed = bins.shape[0] * bins.shape[1]
    message[0:pixels] = ray_code[...]
    message[pixels : pixels + listed] = bins[...].astype(F32).reshape(listed, pixels).astype(BF16)
    message[pixels + listed :] = blank[...]


def tiles_for(most, sizes):
    bounds = [0] + [size for size in sizes if size < most] + [most]
    return [(high, low, high) for low, high in zip(bounds, bounds[1:])]


def layout_kernel(samples, visible, blend, lines, message, before, spread):
    before[...] = (iota(before.shape, 0) < iota(before.shape, 1)).astype(F32).astype(BF16)
    row = iota(spread.shape[1:], 0)
    here = row % samples == iota(spread.shape[1:], 1) // DC
    for k in range(spread.shape[0]):
        mine = here & (row % LISTS // samples == k)
        spread[k] = mine.astype(F32).astype(BF16)
    shares = blend[...] / jnp.sum(blend[...], axis=0, keepdims=True)
    rows = [visible[...].astype(F32)] + parts_of(shares)
    rows.append(jnp.zeros((EXTRA - 4 * visible.shape[0], visible.shape[1]), F32))
    message[message.shape[0] - EXTRA :] = jnp.concatenate(rows, axis=0).astype(BF16)


def lay_out_weights(samples, w_in, w_out, first_w, last_w):
    local_blocks, in_width, hidden = w_in.shape
    for k in range(local_blocks):
        first_w[k, 0:RC] = w_in[k, 0:RC]
        for i in range(RC // DC):
            first_w[k, RC + i * DC : RC + (i + 1) * DC] = w_in[k, RC:]
        wide = jnp.concatenate(
            [
                jnp.broadcast_to(w_out[k, c : c + 1].astype(F32), (samples, hidden))
                for c in range(4)
            ]
            + [jnp.zeros((128 - 4 * samples, hidden), F32)],
            axis=0,
        )
        last_w[k] = wide.T.astype(BF16)


def serve_kernel(own, sources, slots, tiles, *refs):
    messages = refs[:sources]
    if own:
        aside, w_in, w_hid, w_out, table, before, partial, first_w, last_w = refs[
            sources : sources + 9
        ]
    else:
        aside, first_w, w_hid, last_w, table, before, spread, partial, mixed = refs[
            sources : sources + 9
        ]
    places, codes, depths, heads = refs[-4:]
    local_blocks = w_hid.shape[0]
    pixels = messages[0].shape[1]
    lists = messages[0].shape[0] - pixels - EXTRA
    samples = lists // 2
    if own:
        lay_out_weights(samples, w_in, w_out, first_w, last_w)
    first_block = lax.axis_index("block") * local_blocks

    extras = [messages[s][pixels + lists :].astype(F32) for s in range(sources)]

    named = []
    for s in range(sources):
        block = iota((8, pixels), 0)
        known = (block + first_block).astype(F32)
        named.append(
            [
                ((extras[s][v : v + 1] == known) & (block < local_blocks)).astype(F32)
                for v in range(2)
            ]
        )
    either = [first + second for first, second in named]
    ranks = jnp.dot(
        jnp.concatenate(either, axis=0).astype(BF16), before[...], preferred_element_type=F32
    )
    offset = jnp.zeros((8, 1), F32)
    slot_row = iota((slots, pixels), 0).astype(F32)
    for s in range(sources):
        spot = jnp.where(either[s] > 0.0, ranks[8 * s : 8 * s + 8] + offset, -1.0)
        offset = offset + jnp.sum(either[s], axis=1, keepdims=True)
        for k in range(local_blocks):
            places[k * slots : (k + 1) * slots, s * pixels : (s + 1) * pixels] = (
                (slot_row == spot[k : k + 1]).astype(F32).astype(BF16)
            )
    counts = [jnp.max(offset[k : k + 1]).astype(jnp.int32) for k in range(local_blocks)]

    if own:
        spans = [messages[s][0:pixels] for s in range(sources)]
        codes[...] = jnp.dot(
            places[...], jnp.concatenate(spans, axis=0), preferred_element_type=F32
        ).astype(BF16)
        marks_shape = (samples, DC, pixels)
        mark = (iota(marks_shape, 0) * DC + iota(marks_shape, 1)).astype(F32)
        listed = [messages[s][pixels : pixels + lists].astype(F32) for s in range(sources)]
        for k in range(local_blocks):
            marked = []
            for s in range(sources):
                bins = jnp.where(
                    named[s][0][k : k + 1] > 0.0, listed[s][:samples], listed[s][samples:]
                )
                hit = jnp.broadcast_to(bins[:, None, :], marks_shape) == mark
                marked.append(hit.astype(F32).reshape(samples * DC, pixels).astype(BF16))
            rows = slice(k * slots, (k + 1) * slots)
            is_bin = lax.dot_general(
                places[rows],
                jnp.concatenate(marked, axis=1),
                (((1,), (1,)), ((), ())),
                preferred_element_type=F32,
            ).astype(BF16)
            depths[rows] = jnp.dot(is_bin, table[...], preferred_element_type=F32).astype(BF16)
    else:
        lane = iota((pixels, pixels), 1)
        per_turn = pixels // LISTS
        for turn in range(0, sources, per_turn):
            group = []
            for s in range(turn, min(turn + per_turn, sources)):
                bins = messages[s][pixels : pixels + lists].astype(F32)
                for k in range(local_blocks):
                    group.append(
                        jnp.where(named[s][0][k : k + 1] > 0.0, bins[:samples], bins[samples:])
                    )
                group.append(jnp.zeros((LISTS - local_blocks * samples, pixels), F32))
            rows = sum(part.shape[0] for part in group)
            if rows < pixels:
                group.append(jnp.zeros((pixels - rows, pixels), F32))
            turned = jnp.concatenate(group, axis=0).T
            for s in range(turn, min(turn + per_turn, sources)):
                mixed[s * pixels : (s + 1) * pixels, 0:RC] = messages[s][0:pixels]
                mixed[s * pixels : (s + 1) * pixels, RC:] = jnp.where(
                    lane // LISTS == s - turn, turned, 0.0
                ).astype(BF16)

        chosen = jnp.dot(places[...], mixed[...], preferred_element_type=F32).astype(BF16)
        codes[...] = chosen[:, :RC]
        bins = jnp.concatenate(
            [
                jnp.dot(
                    chosen[k * slots : (k + 1) * slots, RC:], spread[k], preferred_element_type=F32
                )
                for k in range(local_blocks)
            ],
            axis=0,
        )
        is_bin = (bins == iota(bins.shape, 1).astype(F32)).astype(F32).astype(BF16)
        depths[...] = jnp.dot(is_bin, table[...], preferred_element_type=F32).astype(BF16)

    heads[...] = jnp.zeros_like(heads)
    per_half = RC // DC
    def one_block(k, carry):
        count = carry[0]
        for i in range(1, local_blocks):
            count = jnp.where(k == i, carry[i], count)

        def one_tile(start, size):
            rows = pl.ds(pl.multiple_of(k * slots + start, 16), size)
            code = codes[rows, :]
            depth = depths[rows, :]
            half_lane = iota((size, RC), 1) // DC
            inputs = []
            for j in range(samples):
                half = depth[:, (j // per_half) * RC : (j // per_half + 1) * RC]
                kept = jnp.where(half_lane == j % per_half, half, jnp.zeros_like(half))
                inputs.append(jnp.concatenate([code, kept], axis=1))
            inputs = jnp.concatenate(inputs, axis=0)
            one = jnp.dot(inputs, first_w[k], preferred_element_type=F32)
            one = jnp.maximum(one, 0.0).astype(BF16)
            two = jnp.dot(one, w_hid[k], preferred_element_type=F32)
            two = jnp.maximum(two, 0.0).astype(BF16)
            out = jnp.dot(two, last_w[k], preferred_element_type=F32)
            sample_lane = iota((size, 128), 1) % samples
            total = jnp.zeros((size, 128), F32)
            for j in range(samples):
                total = jnp.where(sample_lane == j, out[j * size : (j + 1) * size], total)
            heads[rows, :] = total

        for size, fewest, most in tiles:

            @pl.when((count > fewest) & (count <= most))
            def _(size=size):
                one_tile(0, size)

        return carry

    lax.fori_loop(0, local_blocks, one_block, tuple(counts))

    turned = heads[...].T
    optical = jax.nn.softplus(turned[0:samples]) * (1.5 / samples)
    sample_row = iota(optical.shape, 0)
    ahead = jnp.where(sample_row >= 1, pltpu.roll(optical, 1, 0), 0.0)
    step = 1
    while step < samples:
        ahead = ahead + jnp.where(sample_row >= step, pltpu.roll(ahead, step, 0), 0.0)
        step = 2 * step
    weights = jnp.exp(-ahead) * (1.0 - jnp.exp(-optical))
    background = 1.0 - jnp.sum(weights, axis=0, keepdims=True)
    shades = []
    for c in range(1, 4):
        color = jax.nn.sigmoid(turned[c * samples : (c + 1) * samples])
        shades.append(jnp.sum(weights * color, axis=0, keepdims=True) + background)
    shades.append(jnp.zeros_like(background))
    shades = jnp.concatenate(shades, axis=0)[:, : local_blocks * slots]
    stacked = jnp.concatenate(parts_of(shades) + [jnp.zeros_like(shades)], axis=0).astype(BF16)
    sums = [jnp.zeros((3, pixels), F32)] * sources
    for k in range(local_blocks):
        spots = jnp.dot(
            stacked[:, k * slots : (k + 1) * slots],
            places[k * slots : (k + 1) * slots],
            preferred_element_type=F32,
        )
        spots = spots[0:4] + spots[4:8] + spots[8:12]
        for s in range(sources):
            share = jnp.zeros((1, pixels), F32)
            for v in range(2):
                part = extras[s][2 + v : 3 + v] + extras[s][4 + v : 5 + v] + extras[s][6 + v : 7 + v]
                share = share + named[s][v][k : k + 1] * part
            sums[s] = sums[s] + spots[0:3, s * pixels : (s + 1) * pixels] * share
    if own:
        partial[...] = sums[0] - aside[...].reshape(3, pixels)
    else:
        partial[...] = jnp.concatenate([aside[...]] + sums, axis=0)


def gather_kernel(sources, *refs):
    partials = refs[:sources]
    (message,) = refs[sources:]
    pixels = message.shape[1]
    z = lax.axis_index("block")
    squared = jnp.zeros((3, pixels), F32)
    rows = []
    for u in range(sources):
        difference = partials[0][3 * u : 3 * u + 3]
        for t in range(1, sources):
            difference = difference + partials[t][3 * (t ^ u) : 3 * (t ^ u) + 3]
        squared = squared + difference * difference
        rows.append(difference)
    above = jnp.zeros((3, pixels), F32)
    below = jnp.zeros((3, pixels), F32)
    for u in range(1, sources):
        above = above + jnp.where((z ^ u) == z - 1, rows[u], 0.0)
        below = below + jnp.where((z ^ u) == z + 1, rows[u], 0.0)

    def opponent(block, c):
        return sum(OPPONENT[c][i] * block[i : i + 1] for i in range(3) if OPPONENT[c][i])

    mixed = [
        SPREAD[c] * opponent(above, c) + opponent(rows[0], c) + SPREAD[c] * opponent(below, c)
        for c in range(3)
    ]
    total = jnp.sum(jnp.sum(squared, axis=0, keepdims=True), axis=1, keepdims=True)
    message[...] = jnp.concatenate(
        mixed + [jnp.broadcast_to(total, (1, pixels)), rows[0]], axis=0
    )


def finish_kernel(columns, count, *refs):
    messages = refs[:columns]
    truth, rendered, flip_map, psnr = refs[columns:]
    pixels = flip_map.shape[1]
    q = lax.axis_index("rep") * lax.axis_size("tile") + lax.axis_index("tile")
    rendered[...] = messages[0][4:7].reshape(3, 1, pixels) + truth[...]
    own = messages[0][0:4]
    left = jnp.zeros_like(own)
    right = jnp.zeros_like(own)
    total = own[3:4]
    for s in range(1, columns):
        other = messages[s][0:4]
        left = left + jnp.where((q ^ s) == q - 1, other, 0.0)
        right = right + jnp.where((q ^ s) == q + 1, other, 0.0)
        total = total + other[3:4]
    lane = iota(own.shape, 1)
    before = pltpu.roll(jnp.where(lane == pixels - 1, left, own), 1, 1)
    after = pltpu.roll(jnp.where(lane == 0, right, own), pixels - 1, 1)
    summed = jnp.zeros((1, pixels), F32)
    for c in range(3):
        column = SPREAD[c] * before[c : c + 1] + own[c : c + 1] + SPREAD[c] * after[c : c + 1]
        scale = np.float32(1.0) + np.float32(2.0) * np.float32(SPREAD[c])
        emphasised = EMPHASIS[c] * (column / float(scale * scale))
        summed = summed + emphasised * emphasised
    flip_map[...] = jnp.sqrt(summed + 1e-06)
    logged = jnp.log(total / count + 1e-06) * (-10.0 / math.log(10.0))
    psnr[...] = logged[:, 0:1]


def exchange(value, axes, size):
    out = [value]
    for s in range(1, size):
        out.append(lax.ppermute(value, axes, [(i, i ^ s) for i in range(size)]))
    return out


def call(
    kernel, out_shape, in_specs, scratch, flops=0, bytes_accessed=0, limit=8 << 20, aliases=None
):
    cost = None
    if flops:
        cost = pl.CostEstimate(flops=flops, bytes_accessed=bytes_accessed, transcendentals=0)
    return pl.pallas_call(
        kernel,
        out_shape=out_shape,
        in_specs=in_specs,
        scratch_shapes=list(scratch),
        cost_estimate=cost,
        input_output_aliases=aliases or {},
        compiler_params=pltpu.CompilerParams(vmem_limit_bytes=limit),
    )


def body(visible, bins, ray_code, blend, truth, w_in, w_hid, w_out):
    sources = lax.axis_size("block")
    columns = lax.axis_size("rep") * lax.axis_size("tile")
    local_blocks, in_width, hidden = w_in.shape
    pixels = visible.shape[1]
    visible_num = visible.shape[2]
    samples = bins.shape[3]
    blocks_all = local_blocks * sources
    capacity = (2 * pixels * visible_num + blocks_all - 1) // blocks_all
    lists = visible_num * samples
    height = pixels + lists + EXTRA
    far = pl.BlockSpec(memory_space=pltpu.HBM)
    near = pl.BlockSpec(memory_space=pltpu.VMEM)
    blank = call(
        blank_kernel,
        jax.ShapeDtypeStruct((EXTRA, pixels), BF16),
        [],
        (),
        flops=1 << 32,
        bytes_accessed=1 << 17,
    )()
    lines = call(
        pack_kernel, jax.ShapeDtypeStruct((height, pixels), BF16), [near] * 3, ()
    )(
        jnp.transpose(bins.reshape(pixels, visible_num, samples), (1, 2, 0)),
        ray_code.reshape(pixels, RC),
        blank,
    )
    message, before, spread = call(
        functools.partial(layout_kernel, samples),
        (
            jax.ShapeDtypeStruct((height, pixels), BF16),
            jax.ShapeDtypeStruct((pixels, pixels), BF16),
            jax.ShapeDtypeStruct((local_blocks, pixels, samples * DC), BF16),
        ),
        [near] * 3,
        (),
        flops=1 << 32,
        bytes_accessed=1 << 17,
        aliases={2: 0},
    )(visible.reshape(pixels, visible_num).T, blend.reshape(pixels, visible_num).T, lines)
    messages = exchange(message, "block", sources)
    table = jnp.asarray(depth_table(samples))

    def serve(own, parts, aside, weights):
        count = len(parts)
        slots = -(-count * capacity // 16) * 16
        slots_all = local_blocks * slots
        outs = [jax.ShapeDtypeStruct((3 * count + 3 * (not own), pixels), F32)]
        if own:
            outs.append(jax.ShapeDtypeStruct((local_blocks, 2 * RC, hidden), BF16))
            outs.append(jax.ShapeDtypeStruct((local_blocks, hidden, 128), BF16))
        return call(
            functools.partial(
                serve_kernel, own, count, slots, tiles_for(slots, list(range(16, slots, 16)))
            ),
            outs,
            [near] * (count + 6 + (not own)),
            ([] if own else [pltpu.VMEM((count * pixels, 2 * RC), BF16)])
            + [
                pltpu.VMEM((slots_all, count * pixels), BF16),
                pltpu.VMEM((slots_all, RC), BF16),
                pltpu.VMEM((slots_all, samples * DC), BF16),
                pltpu.VMEM((-(-slots_all // 128) * 128, 128), F32),
            ],
            flops=2 * slots_all * samples * hidden * (in_width + hidden + 4),
            bytes_accessed=2 * (w_in.size + w_hid.size),
            limit=40 * 1024 * 1024,
        )(*parts, aside, *weights, table, before, *([] if own else [spread]))

    share, first_w, last_w = serve(True, messages[:1], truth, (w_in, w_hid, w_out))
    (partial,) = serve(False, messages[1:], share, (first_w, w_hid, last_w))
    partials = exchange(partial, "block", sources)
    edge = call(
        functools.partial(gather_kernel, sources),
        jax.ShapeDtypeStruct((7, pixels), F32),
        [near] * sources,
        (),
    )(*partials)
    edges = exchange(edge, ("rep", "tile"), columns)
    rendered, flip_map, psnr = call(
        functools.partial(finish_kernel, columns, 3 * sources * columns * pixels),
        (
            jax.ShapeDtypeStruct((3, 1, pixels), F32),
            jax.ShapeDtypeStruct((1, pixels), F32),
            jax.ShapeDtypeStruct((1, 1), F32),
        ),
        [near] * (columns + 1),
        (),
    )(*edges, truth)
    return (rendered, flip_map, psnr.reshape(1))


def solution(mesh):
    placed = (
        P(("groups", "block"), ("rep", "tile"), None),
        P(("groups", "block"), ("rep", "tile"), None, None),
        P(("groups", "block"), ("rep", "tile"), None),
        P(("groups", "block"), ("rep", "tile"), None),
        P(None, ("groups", "block"), ("rep", "tile")),
        P("block", None, None),
        P("block", None, None),
        P("block", None, None),
    )
    return jax.shard_map(
        body,
        mesh=mesh,
        in_specs=placed,
        out_specs=(
            P(None, ("groups", "block"), ("rep", "tile")),
            P(("groups", "block"), ("rep", "tile")),
            P("groups"),
        ),
        check_vma=False,
    )
```

```python
import functools
import math

import jax
import jax.numpy as jnp
import ml_dtypes
import numpy as np
from jax import lax
from jax.experimental import pallas as pl
from jax.experimental.pallas import tpu as pltpu
from jax.sharding import PartitionSpec as P

RC = 128
DC = 16
NBINS = 256
EXTRA = 16
LISTS = 64

OPPONENT = ((0.2126, 0.7152, 0.0722), (0.5, -0.5, 0.0), (0.0, 0.4, -0.4))
SPREAD = (0.6, 0.35, 0.35)
EMPHASIS = (1.0, 2.0, 2.0)

F32 = jnp.float32
BF16 = jnp.bfloat16


def iota(shape, dim):
    return lax.broadcasted_iota(jnp.int32, shape, dim)


def parts_of(values):
    high = values.astype(BF16).astype(F32)
    rest = values - high
    middle = rest.astype(BF16).astype(F32)
    return [high, middle, rest - middle]


def depth_table(sample_num):
    powers = np.arange(DC // 2, dtype=np.float32)
    steps = (np.float32(np.pi) * np.exp2(powers) / np.float32(NBINS)).astype(np.float32)
    angles = np.arange(NBINS, dtype=np.float32)[:, None] * steps
    wide = angles.astype(np.float64)
    code = np.concatenate([np.sin(wide), np.cos(wide)], axis=1).astype(np.float32)
    stride = NBINS // sample_num
    table = np.zeros((NBINS, sample_num, DC), np.float32)
    for row in range(NBINS):
        table[row, row // stride] = code[row]
    return table.reshape(NBINS, sample_num * DC).astype(ml_dtypes.bfloat16)


def blank_kernel(rows):
    rows[...] = jnp.zeros_like(rows)


def pack_kernel(bins, ray_code, blank, message):
    pixels = ray_code.shape[0]
    listed = bins.shape[0] * bins.shape[1]
    message[0:pixels] = ray_code[...]
    message[pixels : pixels + listed] = bins[...].astype(F32).reshape(listed, pixels).astype(BF16)
    message[pixels + listed :] = blank[...]


def tiles_for(most, sizes):
    bounds = [0] + [size for size in sizes if size < most] + [-(-most // 8) * 8]
    return [(high, low, high) for low, high in zip(bounds, bounds[1:])]


def layout_kernel(samples, visible, blend, lines, message, before, spread):
    before[...] = (iota(before.shape, 0) < iota(before.shape, 1)).astype(F32).astype(BF16)
    row = iota(spread.shape[1:], 0)
    here = row % samples == iota(spread.shape[1:], 1) // DC
    for k in range(spread.shape[0]):
        mine = here & (row % LISTS // samples == k)
        spread[k] = mine.astype(F32).astype(BF16)
    shares = blend[...] / jnp.sum(blend[...], axis=0, keepdims=True)
    rows = [visible[...].astype(F32)] + parts_of(shares)
    rows.append(jnp.zeros((EXTRA - 4 * visible.shape[0], visible.shape[1]), F32))
    message[message.shape[0] - EXTRA :] = jnp.concatenate(rows, axis=0).astype(BF16)


def lay_out_weights(samples, w_in, w_out, first_w, last_w):
    local_blocks, in_width, hidden = w_in.shape
    for k in range(local_blocks):
        first_w[k, 0:RC] = w_in[k, 0:RC]
        for i in range(RC // DC):
            first_w[k, RC + i * DC : RC + (i + 1) * DC] = w_in[k, RC:]
        wide = jnp.concatenate(
            [
                jnp.broadcast_to(w_out[k, c : c + 1].astype(F32), (samples, hidden))
                for c in range(4)
            ]
            + [jnp.zeros((128 - 4 * samples, hidden), F32)],
            axis=0,
        )
        last_w[k] = wide.T.astype(BF16)


def serve_kernel(own, sources, slots, tiles, *refs):
    messages = refs[:sources]
    if own:
        aside, w_in, w_hid, w_out, table, before, partial, first_w, last_w = refs[
            sources : sources + 9
        ]
    else:
        aside, first_w, w_hid, last_w, table, before, spread, partial, mixed = refs[
            sources : sources + 9
        ]
    places, codes, depths, heads = refs[-4:]
    local_blocks = w_hid.shape[0]
    pixels = messages[0].shape[1]
    lists = messages[0].shape[0] - pixels - EXTRA
    samples = lists // 2
    if own:
        lay_out_weights(samples, w_in, w_out, first_w, last_w)
    first_block = lax.axis_index("block") * local_blocks

    extras = [messages[s][pixels + lists :].astype(F32) for s in range(sources)]

    named = []
    for s in range(sources):
        block = iota((8, pixels), 0)
        known = (block + first_block).astype(F32)
        named.append(
            [
                ((extras[s][v : v + 1] == known) & (block < local_blocks)).astype(F32)
                for v in range(2)
            ]
        )
    either = [first + second for first, second in named]
    ranks = jnp.dot(
        jnp.concatenate(either, axis=0).astype(BF16), before[...], preferred_element_type=F32
    )
    offset = jnp.zeros((8, 1), F32)
    slot_row = iota((slots, pixels), 0).astype(F32)
    for s in range(sources):
        spot = jnp.where(either[s] > 0.0, ranks[8 * s : 8 * s + 8] + offset, -1.0)
        offset = offset + jnp.sum(either[s], axis=1, keepdims=True)
        for k in range(local_blocks):
            places[k * slots : (k + 1) * slots, s * pixels : (s + 1) * pixels] = (
                (slot_row == spot[k : k + 1]).astype(F32).astype(BF16)
            )
    counts = [jnp.max(offset[k : k + 1]).astype(jnp.int32) for k in range(local_blocks)]

    if own:
        spans = [messages[s][0:pixels] for s in range(sources)]
        codes[...] = jnp.dot(
            places[...], jnp.concatenate(spans, axis=0), preferred_element_type=F32
        ).astype(BF16)
        marks_shape = (samples, DC, pixels)
        mark = (iota(marks_shape, 0) * DC + iota(marks_shape, 1)).astype(F32)
        listed = [messages[s][pixels : pixels + lists].astype(F32) for s in range(sources)]
        for k in range(local_blocks):
            marked = []
            for s in range(sources):
                bins = jnp.where(
                    named[s][0][k : k + 1] > 0.0, listed[s][:samples], listed[s][samples:]
                )
                hit = jnp.broadcast_to(bins[:, None, :], marks_shape) == mark
                marked.append(hit.astype(F32).reshape(samples * DC, pixels).astype(BF16))
            rows = slice(k * slots, (k + 1) * slots)
            is_bin = lax.dot_general(
                places[rows],
                jnp.concatenate(marked, axis=1),
                (((1,), (1,)), ((), ())),
                preferred_element_type=F32,
            ).astype(BF16)
            depths[rows] = jnp.dot(is_bin, table[...], preferred_element_type=F32).astype(BF16)
    else:
        lane = iota((pixels, pixels), 1)
        per_turn = pixels // LISTS
        for turn in range(0, sources, per_turn):
            group = []
            for s in range(turn, min(turn + per_turn, sources)):
                bins = messages[s][pixels : pixels + lists].astype(F32)
                for k in range(local_blocks):
                    group.append(
                        jnp.where(named[s][0][k : k + 1] > 0.0, bins[:samples], bins[samples:])
                    )
                group.append(jnp.zeros((LISTS - local_blocks * samples, pixels), F32))
            rows = sum(part.shape[0] for part in group)
            if rows < pixels:
                group.append(jnp.zeros((pixels - rows, pixels), F32))
            turned = jnp.concatenate(group, axis=0).T
            for s in range(turn, min(turn + per_turn, sources)):
                mixed[s * pixels : (s + 1) * pixels, 0:RC] = messages[s][0:pixels]
                mixed[s * pixels : (s + 1) * pixels, RC:] = jnp.where(
                    lane // LISTS == s - turn, turned, 0.0
                ).astype(BF16)

        chosen = jnp.dot(places[...], mixed[...], preferred_element_type=F32).astype(BF16)
        codes[...] = chosen[:, :RC]
        bins = jnp.concatenate(
            [
                jnp.dot(
                    chosen[k * slots : (k + 1) * slots, RC:], spread[k], preferred_element_type=F32
                )
                for k in range(local_blocks)
            ],
            axis=0,
        )
        is_bin = (bins == iota(bins.shape, 1).astype(F32)).astype(F32).astype(BF16)
        depths[...] = jnp.dot(is_bin, table[...], preferred_element_type=F32).astype(BF16)

    heads[...] = jnp.zeros_like(heads)
    per_half = RC // DC
    def one_block(k, carry):
        count = carry[0]
        for i in range(1, local_blocks):
            count = jnp.where(k == i, carry[i], count)

        def one_tile(start, size):
            rows = pl.ds(pl.multiple_of(k * slots + start, 16), -(-size // 16) * 16)
            code = codes[rows, :]
            depth = depths[rows, :]
            if size % 16:
                code = code.astype(F32)[:size]
                depth = depth.astype(F32)[:size]
            half_lane = iota((size, RC), 1) // DC
            inputs = []
            for j in range(samples):
                half = depth[:, (j // per_half) * RC : (j // per_half + 1) * RC]
                kept = jnp.where(half_lane == j % per_half, half, jnp.zeros_like(half))
                inputs.append(jnp.concatenate([code, kept], axis=1))
            inputs = jnp.concatenate(inputs, axis=0).astype(BF16)
            one = jnp.dot(inputs, first_w[k], preferred_element_type=F32)
            one = jnp.maximum(one, 0.0).astype(BF16)
            two = jnp.dot(one, w_hid[k], preferred_element_type=F32)
            two = jnp.maximum(two, 0.0).astype(BF16)
            out = jnp.dot(two, last_w[k], preferred_element_type=F32)
            sample_lane = iota((size, 128), 1) % samples
            total = jnp.zeros((size, 128), F32)
            for j in range(samples):
                total = jnp.where(sample_lane == j, out[j * size : (j + 1) * size], total)
            heads[pl.ds(pl.multiple_of(k * slots + start, 16), size), :] = total

        def pick(choices):
            if len(choices) == 1:
                one_tile(0, choices[0][0])
                return
            half = len(choices) // 2
            bound = choices[half - 1][2]

            @pl.when(count <= bound)
            def _():
                pick(choices[:half])

            @pl.when(count > bound)
            def _():
                pick(choices[half:])

        @pl.when(count > 0)
        def _():
            pick(tiles)

        return carry

    lax.fori_loop(0, local_blocks, one_block, tuple(counts))

    turned = heads[...].T
    optical = jax.nn.softplus(turned[0:samples]) * (1.5 / samples)
    sample_row = iota(optical.shape, 0)
    ahead = jnp.where(sample_row >= 1, pltpu.roll(optical, 1, 0), 0.0)
    step = 1
    while step < samples:
        ahead = ahead + jnp.where(sample_row >= step, pltpu.roll(ahead, step, 0), 0.0)
        step = 2 * step
    weights = jnp.exp(-ahead) * (1.0 - jnp.exp(-optical))
    background = 1.0 - jnp.sum(weights, axis=0, keepdims=True)
    shades = []
    for c in range(1, 4):
        color = jax.nn.sigmoid(turned[c * samples : (c + 1) * samples])
        shades.append(jnp.sum(weights * color, axis=0, keepdims=True) + background)
    shades.append(jnp.zeros_like(background))
    shades = jnp.concatenate(shades, axis=0)[:, : local_blocks * slots]
    stacked = jnp.concatenate(parts_of(shades) + [jnp.zeros_like(shades)], axis=0).astype(BF16)
    sums = [jnp.zeros((3, pixels), F32)] * sources
    for k in range(local_blocks):
        spots = jnp.dot(
            stacked[:, k * slots : (k + 1) * slots],
            places[k * slots : (k + 1) * slots],
            preferred_element_type=F32,
        )
        spots = spots[0:4] + spots[4:8] + spots[8:12]
        for s in range(sources):
            share = jnp.zeros((1, pixels), F32)
            for v in range(2):
                part = extras[s][2 + v : 3 + v] + extras[s][4 + v : 5 + v] + extras[s][6 + v : 7 + v]
                share = share + named[s][v][k : k + 1] * part
            sums[s] = sums[s] + spots[0:3, s * pixels : (s + 1) * pixels] * share
    if own:
        partial[...] = sums[0] - aside[...].reshape(3, pixels)
    else:
        partial[...] = jnp.concatenate([aside[...]] + sums, axis=0)


def gather_kernel(sources, *refs):
    partials = refs[:sources]
    (message,) = refs[sources:]
    pixels = message.shape[1]
    z = lax.axis_index("block")
    squared = jnp.zeros((3, pixels), F32)
    rows = []
    for u in range(sources):
        difference = partials[0][3 * u : 3 * u + 3]
        for t in range(1, sources):
            difference = difference + partials[t][3 * (t ^ u) : 3 * (t ^ u) + 3]
        squared = squared + difference * difference
        rows.append(difference)
    above = jnp.zeros((3, pixels), F32)
    below = jnp.zeros((3, pixels), F32)
    for u in range(1, sources):
        above = above + jnp.where((z ^ u) == z - 1, rows[u], 0.0)
        below = below + jnp.where((z ^ u) == z + 1, rows[u], 0.0)

    def opponent(block, c):
        return sum(OPPONENT[c][i] * block[i : i + 1] for i in range(3) if OPPONENT[c][i])

    mixed = [
        SPREAD[c] * opponent(above, c) + opponent(rows[0], c) + SPREAD[c] * opponent(below, c)
        for c in range(3)
    ]
    total = jnp.sum(jnp.sum(squared, axis=0, keepdims=True), axis=1, keepdims=True)
    message[...] = jnp.concatenate(
        mixed + [jnp.broadcast_to(total, (1, pixels)), rows[0]], axis=0
    )


def finish_kernel(columns, count, *refs):
    messages = refs[:columns]
    truth, rendered, flip_map, psnr = refs[columns:]
    pixels = flip_map.shape[1]
    q = lax.axis_index("rep") * lax.axis_size("tile") + lax.axis_index("tile")
    rendered[...] = messages[0][4:7].reshape(3, 1, pixels) + truth[...]
    own = messages[0][0:4]
    left = jnp.zeros_like(own)
    right = jnp.zeros_like(own)
    total = own[3:4]
    for s in range(1, columns):
        other = messages[s][0:4]
        left = left + jnp.where((q ^ s) == q - 1, other, 0.0)
        right = right + jnp.where((q ^ s) == q + 1, other, 0.0)
        total = total + other[3:4]
    lane = iota(own.shape, 1)
    before = pltpu.roll(jnp.where(lane == pixels - 1, left, own), 1, 1)
    after = pltpu.roll(jnp.where(lane == 0, right, own), pixels - 1, 1)
    summed = jnp.zeros((1, pixels), F32)
    for c in range(3):
        column = SPREAD[c] * before[c : c + 1] + own[c : c + 1] + SPREAD[c] * after[c : c + 1]
        scale = np.float32(1.0) + np.float32(2.0) * np.float32(SPREAD[c])
        emphasised = EMPHASIS[c] * (column / float(scale * scale))
        summed = summed + emphasised * emphasised
    flip_map[...] = jnp.sqrt(summed + 1e-06)
    logged = jnp.log(total / count + 1e-06) * (-10.0 / math.log(10.0))
    psnr[...] = logged[:, 0:1]


def exchange(value, axes, size):
    out = [value]
    for s in range(1, size):
        out.append(lax.ppermute(value, axes, [(i, i ^ s) for i in range(size)]))
    return out


def call(
    kernel, out_shape, in_specs, scratch, flops=0, bytes_accessed=0, limit=8 << 20, aliases=None
):
    cost = None
    if flops:
        cost = pl.CostEstimate(flops=flops, bytes_accessed=bytes_accessed, transcendentals=0)
    return pl.pallas_call(
        kernel,
        out_shape=out_shape,
        in_specs=in_specs,
        scratch_shapes=list(scratch),
        cost_estimate=cost,
        input_output_aliases=aliases or {},
        compiler_params=pltpu.CompilerParams(vmem_limit_bytes=limit),
    )


def body(visible, bins, ray_code, blend, truth, w_in, w_hid, w_out):
    sources = lax.axis_size("block")
    columns = lax.axis_size("rep") * lax.axis_size("tile")
    local_blocks, in_width, hidden = w_in.shape
    pixels = visible.shape[1]
    visible_num = visible.shape[2]
    samples = bins.shape[3]
    blocks_all = local_blocks * sources
    capacity = (2 * pixels * visible_num + blocks_all - 1) // blocks_all
    lists = visible_num * samples
    height = pixels + lists + EXTRA
    far = pl.BlockSpec(memory_space=pltpu.HBM)
    near = pl.BlockSpec(memory_space=pltpu.VMEM)
    blank = call(
        blank_kernel,
        jax.ShapeDtypeStruct((EXTRA, pixels), BF16),
        [],
        (),
        flops=1 << 32,
        bytes_accessed=1 << 17,
    )()
    lines = call(
        pack_kernel, jax.ShapeDtypeStruct((height, pixels), BF16), [near] * 3, ()
    )(
        jnp.transpose(bins.reshape(pixels, visible_num, samples), (1, 2, 0)),
        ray_code.reshape(pixels, RC),
        blank,
    )
    message, before, spread = call(
        functools.partial(layout_kernel, samples),
        (
            jax.ShapeDtypeStruct((height, pixels), BF16),
            jax.ShapeDtypeStruct((pixels, pixels), BF16),
            jax.ShapeDtypeStruct((local_blocks, pixels, samples * DC), BF16),
        ),
        [near] * 3,
        (),
        flops=1 << 32,
        bytes_accessed=1 << 17,
        aliases={2: 0},
    )(visible.reshape(pixels, visible_num).T, blend.reshape(pixels, visible_num).T, lines)
    messages = exchange(message, "block", sources)
    table = jnp.asarray(depth_table(samples))

    def serve(own, parts, aside, weights):
        count = len(parts)
        slots = -(-count * capacity // 16) * 16
        slots_all = local_blocks * slots
        outs = [jax.ShapeDtypeStruct((3 * count + 3 * (not own), pixels), F32)]
        if own:
            outs.append(jax.ShapeDtypeStruct((local_blocks, 2 * RC, hidden), BF16))
            outs.append(jax.ShapeDtypeStruct((local_blocks, hidden, 128), BF16))
        return call(
            functools.partial(
                serve_kernel, own, count, slots, tiles_for(count * capacity, list(range(8, slots, 8)))
            ),
            outs,
            [near] * (count + 6 + (not own)),
            ([] if own else [pltpu.VMEM((count * pixels, 2 * RC), BF16)])
            + [
                pltpu.VMEM((slots_all, count * pixels), BF16),
                pltpu.VMEM((slots_all, RC), BF16),
                pltpu.VMEM((slots_all, samples * DC), BF16),
                pltpu.VMEM((-(-slots_all // 128) * 128, 128), F32),
            ],
            flops=2 * slots_all * samples * hidden * (in_width + hidden + 4),
            bytes_accessed=2 * (w_in.size + w_hid.size),
            limit=40 * 1024 * 1024,
        )(*parts, aside, *weights, table, before, *([] if own else [spread]))

    share, first_w, last_w = serve(True, messages[:1], truth, (w_in, w_hid, w_out))
    (partial,) = serve(False, messages[1:], share, (first_w, w_hid, last_w))
    partials = exchange(partial, "block", sources)
    edge = call(
        functools.partial(gather_kernel, sources),
        jax.ShapeDtypeStruct((7, pixels), F32),
        [near] * sources,
        (),
    )(*partials)
    edges = exchange(edge, ("rep", "tile"), columns)
    rendered, flip_map, psnr = call(
        functools.partial(finish_kernel, columns, 3 * sources * columns * pixels),
        (
            jax.ShapeDtypeStruct((3, 1, pixels), F32),
            jax.ShapeDtypeStruct((1, pixels), F32),
            jax.ShapeDtypeStruct((1, 1), F32),
        ),
        [near] * (columns + 1),
        (),
    )(*edges, truth)
    return (rendered, flip_map, psnr.reshape(1))


def solution(mesh):
    placed = (
        P(("groups", "block"), ("rep", "tile"), None),
        P(("groups", "block"), ("rep", "tile"), None, None),
        P(("groups", "block"), ("rep", "tile"), None),
        P(("groups", "block"), ("rep", "tile"), None),
        P(None, ("groups", "block"), ("rep", "tile")),
        P("block", None, None),
        P("block", None, None),
        P("block", None, None),
    )
    return jax.shard_map(
        body,
        mesh=mesh,
        in_specs=placed,
        out_specs=(
            P(None, ("groups", "block"), ("rep", "tile")),
            P(("groups", "block"), ("rep", "tile")),
            P("groups"),
        ),
        check_vma=False,
    )
```

```python
import functools
import math

import jax
import jax.numpy as jnp
import ml_dtypes
import numpy as np
from jax import lax
from jax.experimental import pallas as pl
from jax.experimental.pallas import tpu as pltpu
from jax.sharding import PartitionSpec as P

RC = 128
DC = 16
NBINS = 256
EXTRA = 16
LISTS = 64

OPPONENT = ((0.2126, 0.7152, 0.0722), (0.5, -0.5, 0.0), (0.0, 0.4, -0.4))
SPREAD = (0.6, 0.35, 0.35)
EMPHASIS = (1.0, 2.0, 2.0)

F32 = jnp.float32
BF16 = jnp.bfloat16


def iota(shape, dim):
    return lax.broadcasted_iota(jnp.int32, shape, dim)


def parts_of(values):
    high = values.astype(BF16).astype(F32)
    rest = values - high
    middle = rest.astype(BF16).astype(F32)
    return [high, middle, rest - middle]


def depth_table(sample_num):
    powers = np.arange(DC // 2, dtype=np.float32)
    steps = (np.float32(np.pi) * np.exp2(powers) / np.float32(NBINS)).astype(np.float32)
    angles = np.arange(NBINS, dtype=np.float32)[:, None] * steps
    wide = angles.astype(np.float64)
    code = np.concatenate([np.sin(wide), np.cos(wide)], axis=1).astype(np.float32)
    stride = NBINS // sample_num
    table = np.zeros((NBINS, sample_num, DC), np.float32)
    for row in range(NBINS):
        table[row, row // stride] = code[row]
    return table.reshape(NBINS, sample_num * DC).astype(ml_dtypes.bfloat16)


def layout_kernel(samples, before, spread, blank):
    before[...] = (iota(before.shape, 0) < iota(before.shape, 1)).astype(F32).astype(BF16)
    row = iota(spread.shape[1:], 0)
    here = row % samples == iota(spread.shape[1:], 1) // DC
    for k in range(spread.shape[0]):
        mine = here & (row % LISTS // samples == k)
        spread[k] = mine.astype(F32).astype(BF16)
    blank[...] = jnp.zeros_like(blank)


def pack_kernel(visible, bins, ray_code, blend, blank, message):
    pixels = ray_code.shape[0]
    listed = bins.shape[0] * bins.shape[1]
    message[0:pixels] = ray_code[...]
    message[pixels : pixels + listed] = bins[...].astype(F32).reshape(listed, pixels).astype(BF16)
    shares = blend[...] / jnp.sum(blend[...], axis=0, keepdims=True)
    rows = [visible[...].astype(F32)] + parts_of(shares) + [blank[...]]
    message[pixels + listed :] = jnp.concatenate(rows, axis=0).astype(BF16)


def tiles_for(most, sizes):
    bounds = [0] + [size for size in sizes if size < most] + [-(-most // 8) * 8]
    return [(high, low, high) for low, high in zip(bounds, bounds[1:])]


def lay_out_weights(samples, w_in, w_out, first_w, last_w):
    local_blocks, in_width, hidden = w_in.shape
    for k in range(local_blocks):
        first_w[k, 0:RC] = w_in[k, 0:RC]
        for i in range(RC // DC):
            first_w[k, RC + i * DC : RC + (i + 1) * DC] = w_in[k, RC:]
        wide = jnp.concatenate(
            [
                jnp.broadcast_to(w_out[k, c : c + 1].astype(F32), (samples, hidden))
                for c in range(4)
            ]
            + [jnp.zeros((128 - 4 * samples, hidden), F32)],
            axis=0,
        )
        last_w[k] = wide.T.astype(BF16)


def serve_kernel(own, sources, slots, tiles, *refs):
    messages = refs[:sources]
    if own:
        aside, w_in, w_hid, w_out, table, before, partial, first_w, last_w = refs[
            sources : sources + 9
        ]
    else:
        aside, first_w, w_hid, last_w, table, before, spread, partial, mixed = refs[
            sources : sources + 9
        ]
    places, codes, depths, heads = refs[-4:]
    local_blocks = w_hid.shape[0]
    pixels = messages[0].shape[1]
    lists = messages[0].shape[0] - pixels - EXTRA
    samples = lists // 2
    if own:
        lay_out_weights(samples, w_in, w_out, first_w, last_w)
    first_block = lax.axis_index("block") * local_blocks

    extras = [messages[s][pixels + lists :].astype(F32) for s in range(sources)]

    named = []
    for s in range(sources):
        block = iota((8, pixels), 0)
        known = (block + first_block).astype(F32)
        named.append(
            [
                ((extras[s][v : v + 1] == known) & (block < local_blocks)).astype(F32)
                for v in range(2)
            ]
        )
    either = [first + second for first, second in named]
    ranks = jnp.dot(
        jnp.concatenate(either, axis=0).astype(BF16), before[...], preferred_element_type=F32
    )
    offset = jnp.zeros((8, 1), F32)
    slot_row = iota((slots, pixels), 0).astype(F32)
    for s in range(sources):
        spot = jnp.where(either[s] > 0.0, ranks[8 * s : 8 * s + 8] + offset, -1.0)
        offset = offset + jnp.sum(either[s], axis=1, keepdims=True)
        for k in range(local_blocks):
            places[k * slots : (k + 1) * slots, s * pixels : (s + 1) * pixels] = (
                (slot_row == spot[k : k + 1]).astype(F32).astype(BF16)
            )
    counts = [jnp.max(offset[k : k + 1]).astype(jnp.int32) for k in range(local_blocks)]

    if own:
        spans = [messages[s][0:pixels] for s in range(sources)]
        codes[...] = jnp.dot(
            places[...], jnp.concatenate(spans, axis=0), preferred_element_type=F32
        ).astype(BF16)
        marks_shape = (samples, DC, pixels)
        mark = (iota(marks_shape, 0) * DC + iota(marks_shape, 1)).astype(F32)
        listed = [messages[s][pixels : pixels + lists].astype(F32) for s in range(sources)]
        for k in range(local_blocks):
            marked = []
            for s in range(sources):
                bins = jnp.where(
                    named[s][0][k : k + 1] > 0.0, listed[s][:samples], listed[s][samples:]
                )
                hit = jnp.broadcast_to(bins[:, None, :], marks_shape) == mark
                marked.append(hit.astype(F32).reshape(samples * DC, pixels).astype(BF16))
            rows = slice(k * slots, (k + 1) * slots)
            is_bin = lax.dot_general(
                places[rows],
                jnp.concatenate(marked, axis=1),
                (((1,), (1,)), ((), ())),
                preferred_element_type=F32,
            ).astype(BF16)
            depths[rows] = jnp.dot(is_bin, table[...], preferred_element_type=F32).astype(BF16)
    else:
        lane = iota((pixels, pixels), 1)
        per_turn = pixels // LISTS
        for turn in range(0, sources, per_turn):
            group = []
            for s in range(turn, min(turn + per_turn, sources)):
                bins = messages[s][pixels : pixels + lists].astype(F32)
                for k in range(local_blocks):
                    group.append(
                        jnp.where(named[s][0][k : k + 1] > 0.0, bins[:samples], bins[samples:])
                    )
                group.append(jnp.zeros((LISTS - local_blocks * samples, pixels), F32))
            rows = sum(part.shape[0] for part in group)
            if rows < pixels:
                group.append(jnp.zeros((pixels - rows, pixels), F32))
            turned = jnp.concatenate(group, axis=0).T
            for s in range(turn, min(turn + per_turn, sources)):
                mixed[s * pixels : (s + 1) * pixels, 0:RC] = messages[s][0:pixels]
                mixed[s * pixels : (s + 1) * pixels, RC:] = jnp.where(
                    lane // LISTS == s - turn, turned, 0.0
                ).astype(BF16)

        chosen = jnp.dot(places[...], mixed[...], preferred_element_type=F32).astype(BF16)
        codes[...] = chosen[:, :RC]
        bins = jnp.concatenate(
            [
                jnp.dot(
                    chosen[k * slots : (k + 1) * slots, RC:], spread[k], preferred_element_type=F32
                )
                for k in range(local_blocks)
            ],
            axis=0,
        )
        is_bin = (bins == iota(bins.shape, 1).astype(F32)).astype(F32).astype(BF16)
        depths[...] = jnp.dot(is_bin, table[...], preferred_element_type=F32).astype(BF16)

    heads[...] = jnp.zeros_like(heads)
    per_half = RC // DC
    def one_block(k, carry):
        count = carry[0]
        for i in range(1, local_blocks):
            count = jnp.where(k == i, carry[i], count)

        def one_tile(start, size):
            rows = pl.ds(pl.multiple_of(k * slots + start, 16), -(-size // 16) * 16)
            code = codes[rows, :]
            depth = depths[rows, :]
            if size % 16:
                code = code.astype(F32)[:size]
                depth = depth.astype(F32)[:size]
            half_lane = iota((size, RC), 1) // DC
            inputs = []
            for j in range(samples):
                half = depth[:, (j // per_half) * RC : (j // per_half + 1) * RC]
                kept = jnp.where(half_lane == j % per_half, half, jnp.zeros_like(half))
                inputs.append(jnp.concatenate([code, kept], axis=1))
            inputs = jnp.concatenate(inputs, axis=0).astype(BF16)
            one = jnp.dot(inputs, first_w[k], preferred_element_type=F32)
            one = jnp.maximum(one, 0.0).astype(BF16)
            two = jnp.dot(one, w_hid[k], preferred_element_type=F32)
            two = jnp.maximum(two, 0.0).astype(BF16)
            out = jnp.dot(two, last_w[k], preferred_element_type=F32)
            sample_lane = iota((size, 128), 1) % samples
            total = jnp.zeros((size, 128), F32)
            for j in range(samples):
                total = jnp.where(sample_lane == j, out[j * size : (j + 1) * size], total)
            heads[pl.ds(pl.multiple_of(k * slots + start, 16), size), :] = total

        def pick(choices):
            if len(choices) == 1:
                one_tile(0, choices[0][0])
                return
            half = len(choices) // 2
            bound = choices[half - 1][2]

            @pl.when(count <= bound)
            def _():
                pick(choices[:half])

            @pl.when(count > bound)
            def _():
                pick(choices[half:])

        @pl.when(count > 0)
        def _():
            pick(tiles)

        return carry

    lax.fori_loop(0, local_blocks, one_block, tuple(counts))

    turned = heads[...].T
    optical = jax.nn.softplus(turned[0:samples]) * (1.5 / samples)
    sample_row = iota(optical.shape, 0)
    ahead = jnp.where(sample_row >= 1, pltpu.roll(optical, 1, 0), 0.0)
    step = 1
    while step < samples:
        ahead = ahead + jnp.where(sample_row >= step, pltpu.roll(ahead, step, 0), 0.0)
        step = 2 * step
    weights = jnp.exp(-ahead) * (1.0 - jnp.exp(-optical))
    background = 1.0 - jnp.sum(weights, axis=0, keepdims=True)
    shades = []
    for c in range(1, 4):
        color = jax.nn.sigmoid(turned[c * samples : (c + 1) * samples])
        shades.append(jnp.sum(weights * color, axis=0, keepdims=True) + background)
    shades.append(jnp.zeros_like(background))
    shades = jnp.concatenate(shades, axis=0)[:, : local_blocks * slots]
    stacked = jnp.concatenate(parts_of(shades) + [jnp.zeros_like(shades)], axis=0).astype(BF16)
    sums = [jnp.zeros((3, pixels), F32)] * sources
    for k in range(local_blocks):
        spots = jnp.dot(
            stacked[:, k * slots : (k + 1) * slots],
            places[k * slots : (k + 1) * slots],
            preferred_element_type=F32,
        )
        spots = spots[0:4] + spots[4:8] + spots[8:12]
        for s in range(sources):
            share = jnp.zeros((1, pixels), F32)
            for v in range(2):
                part = extras[s][2 + v : 3 + v] + extras[s][4 + v : 5 + v] + extras[s][6 + v : 7 + v]
                share = share + named[s][v][k : k + 1] * part
            sums[s] = sums[s] + spots[0:3, s * pixels : (s + 1) * pixels] * share
    if own:
        partial[...] = sums[0] - aside[...].reshape(3, pixels)
    else:
        partial[...] = jnp.concatenate([aside[...]] + sums, axis=0)


def gather_kernel(sources, *refs):
    partials = refs[:sources]
    (message,) = refs[sources:]
    pixels = message.shape[1]
    z = lax.axis_index("block")
    squared = jnp.zeros((3, pixels), F32)
    rows = []
    for u in range(sources):
        difference = partials[0][3 * u : 3 * u + 3]
        for t in range(1, sources):
            difference = difference + partials[t][3 * (t ^ u) : 3 * (t ^ u) + 3]
        squared = squared + difference * difference
        rows.append(difference)
    above = jnp.zeros((3, pixels), F32)
    below = jnp.zeros((3, pixels), F32)
    for u in range(1, sources):
        above = above + jnp.where((z ^ u) == z - 1, rows[u], 0.0)
        below = below + jnp.where((z ^ u) == z + 1, rows[u], 0.0)

    def opponent(block, c):
        return sum(OPPONENT[c][i] * block[i : i + 1] for i in range(3) if OPPONENT[c][i])

    mixed = [
        SPREAD[c] * opponent(above, c) + opponent(rows[0], c) + SPREAD[c] * opponent(below, c)
        for c in range(3)
    ]
    total = jnp.sum(jnp.sum(squared, axis=0, keepdims=True), axis=1, keepdims=True)
    message[...] = jnp.concatenate(
        mixed + [jnp.broadcast_to(total, (1, pixels)), rows[0]], axis=0
    )


def finish_kernel(columns, count, *refs):
    messages = refs[:columns]
    truth, rendered, flip_map, psnr = refs[columns:]
    pixels = flip_map.shape[1]
    q = lax.axis_index("rep") * lax.axis_size("tile") + lax.axis_index("tile")
    rendered[...] = messages[0][4:7].reshape(3, 1, pixels) + truth[...]
    own = messages[0][0:4]
    left = jnp.zeros_like(own)
    right = jnp.zeros_like(own)
    total = own[3:4]
    for s in range(1, columns):
        other = messages[s][0:4]
        left = left + jnp.where((q ^ s) == q - 1, other, 0.0)
        right = right + jnp.where((q ^ s) == q + 1, other, 0.0)
        total = total + other[3:4]
    lane = iota(own.shape, 1)
    before = pltpu.roll(jnp.where(lane == pixels - 1, left, own), 1, 1)
    after = pltpu.roll(jnp.where(lane == 0, right, own), pixels - 1, 1)
    summed = jnp.zeros((1, pixels), F32)
    for c in range(3):
        column = SPREAD[c] * before[c : c + 1] + own[c : c + 1] + SPREAD[c] * after[c : c + 1]
        scale = np.float32(1.0) + np.float32(2.0) * np.float32(SPREAD[c])
        emphasised = EMPHASIS[c] * (column / float(scale * scale))
        summed = summed + emphasised * emphasised
    flip_map[...] = jnp.sqrt(summed + 1e-06)
    logged = jnp.log(total / count + 1e-06) * (-10.0 / math.log(10.0))
    psnr[...] = logged[:, 0:1]


def exchange(value, axes, size):
    out = [value]
    for s in range(1, size):
        out.append(lax.ppermute(value, axes, [(i, i ^ s) for i in range(size)]))
    return out


def call(
    kernel, out_shape, in_specs, scratch, flops=0, bytes_accessed=0, limit=8 << 20
):
    cost = None
    if flops:
        cost = pl.CostEstimate(flops=flops, bytes_accessed=bytes_accessed, transcendentals=0)
    return pl.pallas_call(
        kernel,
        out_shape=out_shape,
        in_specs=in_specs,
        scratch_shapes=list(scratch),
        cost_estimate=cost,
        compiler_params=pltpu.CompilerParams(vmem_limit_bytes=limit),
    )


def body(visible, bins, ray_code, blend, truth, w_in, w_hid, w_out):
    sources = lax.axis_size("block")
    columns = lax.axis_size("rep") * lax.axis_size("tile")
    local_blocks, in_width, hidden = w_in.shape
    pixels = visible.shape[1]
    visible_num = visible.shape[2]
    samples = bins.shape[3]
    blocks_all = local_blocks * sources
    capacity = (2 * pixels * visible_num + blocks_all - 1) // blocks_all
    lists = visible_num * samples
    height = pixels + lists + EXTRA
    far = pl.BlockSpec(memory_space=pltpu.HBM)
    near = pl.BlockSpec(memory_space=pltpu.VMEM)
    before, spread, blank = call(
        functools.partial(layout_kernel, samples),
        (
            jax.ShapeDtypeStruct((pixels, pixels), BF16),
            jax.ShapeDtypeStruct((local_blocks, pixels, samples * DC), BF16),
            jax.ShapeDtypeStruct((EXTRA - 4 * visible_num, pixels), F32),
        ),
        [],
        (),
        flops=1 << 32,
        bytes_accessed=1 << 17,
    )()
    message = call(
        pack_kernel,
        jax.ShapeDtypeStruct((height, pixels), BF16),
        [near] * 5,
        (),
        flops=1 << 32,
        bytes_accessed=1 << 17,
    )(
        visible.reshape(pixels, visible_num).T,
        jnp.transpose(bins.reshape(pixels, visible_num, samples), (1, 2, 0)),
        ray_code.reshape(pixels, RC),
        blend.reshape(pixels, visible_num).T,
        blank,
    )
    messages = exchange(message, "block", sources)
    table = jnp.asarray(depth_table(samples))

    def serve(own, parts, aside, weights):
        count = len(parts)
        slots = -(-count * capacity // 16) * 16
        slots_all = local_blocks * slots
        outs = [jax.ShapeDtypeStruct((3 * count + 3 * (not own), pixels), F32)]
        if own:
            outs.append(jax.ShapeDtypeStruct((local_blocks, 2 * RC, hidden), BF16))
            outs.append(jax.ShapeDtypeStruct((local_blocks, hidden, 128), BF16))
        return call(
            functools.partial(
                serve_kernel, own, count, slots, tiles_for(count * capacity, list(range(8, slots, 8)))
            ),
            outs,
            [near] * (count + 6 + (not own)),
            ([] if own else [pltpu.VMEM((count * pixels, 2 * RC), BF16)])
            + [
                pltpu.VMEM((slots_all, count * pixels), BF16),
                pltpu.VMEM((slots_all, RC), BF16),
                pltpu.VMEM((slots_all, samples * DC), BF16),
                pltpu.VMEM((-(-slots_all // 128) * 128, 128), F32),
            ],
            flops=2 * slots_all * samples * hidden * (in_width + hidden + 4),
            bytes_accessed=2 * (w_in.size + w_hid.size),
            limit=40 * 1024 * 1024,
        )(*parts, aside, *weights, table, before, *([] if own else [spread]))

    share, first_w, last_w = serve(True, messages[:1], truth, (w_in, w_hid, w_out))
    (partial,) = serve(False, messages[1:], share, (first_w, w_hid, last_w))
    partials = exchange(partial, "block", sources)
    edge = call(
        functools.partial(gather_kernel, sources),
        jax.ShapeDtypeStruct((7, pixels), F32),
        [near] * sources,
        (),
    )(*partials)
    edges = exchange(edge, ("rep", "tile"), columns)
    rendered, flip_map, psnr = call(
        functools.partial(finish_kernel, columns, 3 * sources * columns * pixels),
        (
            jax.ShapeDtypeStruct((3, 1, pixels), F32),
            jax.ShapeDtypeStruct((1, pixels), F32),
            jax.ShapeDtypeStruct((1, 1), F32),
        ),
        [near] * (columns + 1),
        (),
    )(*edges, truth)
    return (rendered, flip_map, psnr.reshape(1))


def solution(mesh):
    placed = (
        P(("groups", "block"), ("rep", "tile"), None),
        P(("groups", "block"), ("rep", "tile"), None, None),
        P(("groups", "block"), ("rep", "tile"), None),
        P(("groups", "block"), ("rep", "tile"), None),
        P(None, ("groups", "block"), ("rep", "tile")),
        P("block", None, None),
        P("block", None, None),
        P("block", None, None),
    )
    return jax.shard_map(
        body,
        mesh=mesh,
        in_specs=placed,
        out_specs=(
            P(None, ("groups", "block"), ("rep", "tile")),
            P(("groups", "block"), ("rep", "tile")),
            P("groups"),
        ),
        check_vma=False,
    )
```

```python
import functools
import math

import jax
import jax.numpy as jnp
import ml_dtypes
import numpy as np
from jax import lax
from jax.experimental import pallas as pl
from jax.experimental.pallas import tpu as pltpu
from jax.sharding import PartitionSpec as P

RC = 128
DC = 16
NBINS = 256
EXTRA = 16
LISTS = 64

OPPONENT = ((0.2126, 0.7152, 0.0722), (0.5, -0.5, 0.0), (0.0, 0.4, -0.4))
SPREAD = (0.6, 0.35, 0.35)
EMPHASIS = (1.0, 2.0, 2.0)

F32 = jnp.float32
BF16 = jnp.bfloat16


def iota(shape, dim):
    return lax.broadcasted_iota(jnp.int32, shape, dim)


def parts_of(values):
    high = values.astype(BF16).astype(F32)
    rest = values - high
    middle = rest.astype(BF16).astype(F32)
    return [high, middle, rest - middle]


def depth_table(sample_num):
    powers = np.arange(DC // 2, dtype=np.float32)
    steps = (np.float32(np.pi) * np.exp2(powers) / np.float32(NBINS)).astype(np.float32)
    angles = np.arange(NBINS, dtype=np.float32)[:, None] * steps
    wide = angles.astype(np.float64)
    code = np.concatenate([np.sin(wide), np.cos(wide)], axis=1).astype(np.float32)
    stride = NBINS // sample_num
    table = np.zeros((NBINS, sample_num, DC), np.float32)
    for row in range(NBINS):
        table[row, row // stride] = code[row]
    return table.reshape(NBINS, sample_num * DC).astype(ml_dtypes.bfloat16)


def layout_kernel(samples, before, spread, blank):
    before[...] = (iota(before.shape, 0) < iota(before.shape, 1)).astype(F32).astype(BF16)
    row = iota(spread.shape[1:], 0)
    here = row % samples == iota(spread.shape[1:], 1) // DC
    for k in range(spread.shape[0]):
        mine = here & (row % LISTS // samples == k)
        spread[k] = mine.astype(F32).astype(BF16)
    blank[...] = jnp.zeros_like(blank)


def pack_kernel(visible, bins, ray_code, blend, blank, message):
    pixels = ray_code.shape[0]
    listed = bins.shape[0] * bins.shape[1]
    message[0:pixels] = ray_code[...]
    message[pixels : pixels + listed] = bins[...].astype(F32).reshape(listed, pixels).astype(BF16)
    shares = blend[...] / jnp.sum(blend[...], axis=0, keepdims=True)
    rows = [visible[...].astype(F32)] + parts_of(shares) + [blank[...]]
    message[pixels + listed :] = jnp.concatenate(rows, axis=0).astype(BF16)


def tiles_for(most, sizes):
    bounds = [0] + [size for size in sizes if size < most] + [-(-most // 8) * 8]
    return [(high, low, high) for low, high in zip(bounds, bounds[1:])]


def lay_out_weights(samples, w_in, w_out, first_w, last_w):
    local_blocks, in_width, hidden = w_in.shape
    for k in range(local_blocks):
        first_w[k, 0:RC] = w_in[k, 0:RC]
        for i in range(RC // DC):
            first_w[k, RC + i * DC : RC + (i + 1) * DC] = w_in[k, RC:]
        wide = jnp.concatenate(
            [
                jnp.broadcast_to(w_out[k, c : c + 1].astype(F32), (samples, hidden))
                for c in range(4)
            ]
            + [jnp.zeros((128 - 4 * samples, hidden), F32)],
            axis=0,
        )
        last_w[k] = wide.T.astype(BF16)


def serve_kernel(own, sources, slots, tiles, *refs):
    messages = refs[:sources]
    if own:
        aside, w_in, w_hid, w_out, table, before, partial, first_w, last_w = refs[
            sources : sources + 9
        ]
    else:
        aside, first_w, w_hid, last_w, table, before, spread, partial, mixed = refs[
            sources : sources + 9
        ]
    places, codes, depths, heads = refs[-4:]
    local_blocks = w_hid.shape[0]
    pixels = messages[0].shape[1]
    lists = messages[0].shape[0] - pixels - EXTRA
    samples = lists // 2
    if own:
        lay_out_weights(samples, w_in, w_out, first_w, last_w)
    first_block = lax.axis_index("block") * local_blocks

    extras = [messages[s][pixels + lists :].astype(F32) for s in range(sources)]

    named = []
    for s in range(sources):
        block = iota((8, pixels), 0)
        known = (block + first_block).astype(F32)
        named.append(
            [
                ((extras[s][v : v + 1] == known) & (block < local_blocks)).astype(F32)
                for v in range(2)
            ]
        )
    either = [first + second for first, second in named]
    ranks = jnp.dot(
        jnp.concatenate(either, axis=0).astype(BF16), before[...], preferred_element_type=F32
    )
    offset = jnp.zeros((8, 1), F32)
    slot_row = iota((slots, pixels), 0).astype(F32)
    for s in range(sources):
        spot = jnp.where(either[s] > 0.0, ranks[8 * s : 8 * s + 8] + offset, -1.0)
        offset = offset + jnp.sum(either[s], axis=1, keepdims=True)
        for k in range(local_blocks):
            places[k * slots : (k + 1) * slots, s * pixels : (s + 1) * pixels] = (
                (slot_row == spot[k : k + 1]).astype(F32).astype(BF16)
            )
    counts = [jnp.max(offset[k : k + 1]).astype(jnp.int32) for k in range(local_blocks)]

    if own:
        spans = [messages[s][0:pixels] for s in range(sources)]
        codes[...] = jnp.dot(
            places[...], jnp.concatenate(spans, axis=0), preferred_element_type=F32
        ).astype(BF16)
        marks_shape = (samples, DC, pixels)
        mark = (iota(marks_shape, 0) * DC + iota(marks_shape, 1)).astype(F32)
        listed = [messages[s][pixels : pixels + lists].astype(F32) for s in range(sources)]
        for k in range(local_blocks):
            marked = []
            for s in range(sources):
                bins = jnp.where(
                    named[s][0][k : k + 1] > 0.0, listed[s][:samples], listed[s][samples:]
                )
                hit = jnp.broadcast_to(bins[:, None, :], marks_shape) == mark
                marked.append(hit.astype(F32).reshape(samples * DC, pixels).astype(BF16))
            rows = slice(k * slots, (k + 1) * slots)
            is_bin = lax.dot_general(
                places[rows],
                jnp.concatenate(marked, axis=1),
                (((1,), (1,)), ((), ())),
                preferred_element_type=F32,
            ).astype(BF16)
            depths[rows] = jnp.dot(is_bin, table[...], preferred_element_type=F32).astype(BF16)
    else:
        lane = iota((pixels, pixels), 1)
        per_turn = pixels // LISTS
        for turn in range(0, sources, per_turn):
            group = []
            for s in range(turn, min(turn + per_turn, sources)):
                bins = messages[s][pixels : pixels + lists].astype(F32)
                for k in range(local_blocks):
                    group.append(
                        jnp.where(named[s][0][k : k + 1] > 0.0, bins[:samples], bins[samples:])
                    )
                group.append(jnp.zeros((LISTS - local_blocks * samples, pixels), F32))
            rows = sum(part.shape[0] for part in group)
            if rows < pixels:
                group.append(jnp.zeros((pixels - rows, pixels), F32))
            turned = jnp.concatenate(group, axis=0).T
            for s in range(turn, min(turn + per_turn, sources)):
                mixed[s * pixels : (s + 1) * pixels, 0:RC] = messages[s][0:pixels]
                mixed[s * pixels : (s + 1) * pixels, RC:] = jnp.where(
                    lane // LISTS == s - turn, turned, 0.0
                ).astype(BF16)

        chosen = jnp.dot(places[...], mixed[...], preferred_element_type=F32).astype(BF16)
        codes[...] = chosen[:, :RC]
        bins = jnp.concatenate(
            [
                jnp.dot(
                    chosen[k * slots : (k + 1) * slots, RC:], spread[k], preferred_element_type=F32
                )
                for k in range(local_blocks)
            ],
            axis=0,
        )
        is_bin = (bins == iota(bins.shape, 1).astype(F32)).astype(F32).astype(BF16)
        depths[...] = jnp.dot(is_bin, table[...], preferred_element_type=F32).astype(BF16)

    heads[...] = jnp.zeros_like(heads)
    per_half = RC // DC
    def one_block(k, carry):
        count = carry[0]
        for i in range(1, local_blocks):
            count = jnp.where(k == i, carry[i], count)

        def one_tile(start, size):
            rows = pl.ds(pl.multiple_of(k * slots + start, 16), -(-size // 16) * 16)
            code = codes[rows, :]
            depth = depths[rows, :]
            if size % 16:
                code = code.astype(F32)[:size]
                depth = depth.astype(F32)[:size]
            half_lane = iota((size, RC), 1) // DC
            inputs = []
            for j in range(samples):
                half = depth[:, (j // per_half) * RC : (j // per_half + 1) * RC]
                kept = jnp.where(half_lane == j % per_half, half, jnp.zeros_like(half))
                inputs.append(jnp.concatenate([code, kept], axis=1))
            inputs = jnp.concatenate(inputs, axis=0).astype(BF16)
            one = jnp.dot(inputs, first_w[k], preferred_element_type=F32)
            one = jnp.maximum(one, 0.0).astype(BF16)
            two = jnp.dot(one, w_hid[k], preferred_element_type=F32)
            two = jnp.maximum(two, 0.0).astype(BF16)
            out = jnp.dot(two, last_w[k], preferred_element_type=F32)
            sample_lane = iota((size, 128), 1) % samples
            total = jnp.zeros((size, 128), F32)
            for j in range(samples):
                total = jnp.where(sample_lane == j, out[j * size : (j + 1) * size], total)
            heads[pl.ds(pl.multiple_of(k * slots + start, 16), size), :] = total

        def pick(choices):
            if len(choices) == 1:
                one_tile(0, choices[0][0])
                return
            half = len(choices) // 2
            bound = choices[half - 1][2]

            @pl.when(count <= bound)
            def _():
                pick(choices[:half])

            @pl.when(count > bound)
            def _():
                pick(choices[half:])

        @pl.when(count > 0)
        def _():
            pick(tiles)

        return carry

    lax.fori_loop(0, local_blocks, one_block, tuple(counts))

    turned = heads[...].T
    optical = jax.nn.softplus(turned[0:samples]) * (1.5 / samples)
    sample_row = iota(optical.shape, 0)
    ahead = jnp.where(sample_row >= 1, pltpu.roll(optical, 1, 0), 0.0)
    step = 1
    while step < samples:
        ahead = ahead + jnp.where(sample_row >= step, pltpu.roll(ahead, step, 0), 0.0)
        step = 2 * step
    weights = jnp.exp(-ahead) * (1.0 - jnp.exp(-optical))
    background = 1.0 - jnp.sum(weights, axis=0, keepdims=True)
    shades = []
    for c in range(1, 4):
        color = jax.nn.sigmoid(turned[c * samples : (c + 1) * samples])
        shades.append(jnp.sum(weights * color, axis=0, keepdims=True) + background)
    shades.append(jnp.zeros_like(background))
    shades = jnp.concatenate(shades, axis=0)[:, : local_blocks * slots]
    stacked = jnp.concatenate(parts_of(shades) + [jnp.zeros_like(shades)], axis=0).astype(BF16)
    sums = [jnp.zeros((3, pixels), F32)] * sources
    for k in range(local_blocks):
        spots = jnp.dot(
            stacked[:, k * slots : (k + 1) * slots],
            places[k * slots : (k + 1) * slots],
            preferred_element_type=F32,
        )
        spots = spots[0:4] + spots[4:8] + spots[8:12]
        for s in range(sources):
            share = jnp.zeros((1, pixels), F32)
            for v in range(2):
                part = extras[s][2 + v : 3 + v] + extras[s][4 + v : 5 + v] + extras[s][6 + v : 7 + v]
                share = share + named[s][v][k : k + 1] * part
            sums[s] = sums[s] + spots[0:3, s * pixels : (s + 1) * pixels] * share
    if own:
        partial[...] = sums[0] - aside[...].reshape(3, pixels)
    else:
        partial[...] = jnp.concatenate([aside[...]] + sums, axis=0)


def gather_kernel(sources, *refs):
    partials = refs[:sources]
    message, errors = refs[sources:]
    pixels = message.shape[1]
    z = lax.axis_index("block")
    squared = jnp.zeros((3, pixels), F32)
    rows = []
    for u in range(sources):
        difference = partials[0][3 * u : 3 * u + 3]
        for t in range(1, sources):
            difference = difference + partials[t][3 * (t ^ u) : 3 * (t ^ u) + 3]
        squared = squared + difference * difference
        rows.append(difference)
    above = jnp.zeros((3, pixels), F32)
    below = jnp.zeros((3, pixels), F32)
    for u in range(1, sources):
        above = above + jnp.where((z ^ u) == z - 1, rows[u], 0.0)
        below = below + jnp.where((z ^ u) == z + 1, rows[u], 0.0)

    def opponent(block, c):
        return sum(OPPONENT[c][i] * block[i : i + 1] for i in range(3) if OPPONENT[c][i])

    mixed = [
        SPREAD[c] * opponent(above, c) + opponent(rows[0], c) + SPREAD[c] * opponent(below, c)
        for c in range(3)
    ]
    total = jnp.sum(jnp.sum(squared, axis=0, keepdims=True), axis=1, keepdims=True)
    message[...] = jnp.concatenate(mixed + [jnp.broadcast_to(total, (1, pixels))], axis=0)
    errors[...] = rows[0]


def finish_kernel(columns, count, *refs):
    messages = refs[:columns]
    errors, truth, rendered, flip_map, psnr = refs[columns:]
    pixels = flip_map.shape[1]
    q = lax.axis_index("rep") * lax.axis_size("tile") + lax.axis_index("tile")
    rendered[...] = errors[...].reshape(3, 1, pixels) + truth[...]
    own = messages[0][...]
    left = jnp.zeros_like(own)
    right = jnp.zeros_like(own)
    total = own[3:4]
    for s in range(1, columns):
        other = messages[s][...]
        left = left + jnp.where((q ^ s) == q - 1, other, 0.0)
        right = right + jnp.where((q ^ s) == q + 1, other, 0.0)
        total = total + other[3:4]
    lane = iota(own.shape, 1)
    before = pltpu.roll(jnp.where(lane == pixels - 1, left, own), 1, 1)
    after = pltpu.roll(jnp.where(lane == 0, right, own), pixels - 1, 1)
    summed = jnp.zeros((1, pixels), F32)
    for c in range(3):
        column = SPREAD[c] * before[c : c + 1] + own[c : c + 1] + SPREAD[c] * after[c : c + 1]
        scale = np.float32(1.0) + np.float32(2.0) * np.float32(SPREAD[c])
        emphasised = EMPHASIS[c] * (column / float(scale * scale))
        summed = summed + emphasised * emphasised
    flip_map[...] = jnp.sqrt(summed + 1e-06)
    logged = jnp.log(total / count + 1e-06) * (-10.0 / math.log(10.0))
    psnr[...] = logged[:, 0:1]


def exchange(value, axes, size):
    out = [value]
    for s in range(1, size):
        out.append(lax.ppermute(value, axes, [(i, i ^ s) for i in range(size)]))
    return out


def call(
    kernel, out_shape, in_specs, scratch, flops=0, bytes_accessed=0, limit=8 << 20
):
    cost = None
    if flops:
        cost = pl.CostEstimate(flops=flops, bytes_accessed=bytes_accessed, transcendentals=0)
    return pl.pallas_call(
        kernel,
        out_shape=out_shape,
        in_specs=in_specs,
        scratch_shapes=list(scratch),
        cost_estimate=cost,
        compiler_params=pltpu.CompilerParams(vmem_limit_bytes=limit),
    )


def body(visible, bins, ray_code, blend, truth, w_in, w_hid, w_out):
    sources = lax.axis_size("block")
    columns = lax.axis_size("rep") * lax.axis_size("tile")
    local_blocks, in_width, hidden = w_in.shape
    pixels = visible.shape[1]
    visible_num = visible.shape[2]
    samples = bins.shape[3]
    blocks_all = local_blocks * sources
    capacity = (2 * pixels * visible_num + blocks_all - 1) // blocks_all
    lists = visible_num * samples
    height = pixels + lists + EXTRA
    far = pl.BlockSpec(memory_space=pltpu.HBM)
    near = pl.BlockSpec(memory_space=pltpu.VMEM)
    before, spread, blank = call(
        functools.partial(layout_kernel, samples),
        (
            jax.ShapeDtypeStruct((pixels, pixels), BF16),
            jax.ShapeDtypeStruct((local_blocks, pixels, samples * DC), BF16),
            jax.ShapeDtypeStruct((EXTRA - 4 * visible_num, pixels), F32),
        ),
        [],
        (),
        flops=1 << 32,
        bytes_accessed=1 << 17,
    )()
    message = call(
        pack_kernel,
        jax.ShapeDtypeStruct((height, pixels), BF16),
        [near] * 5,
        (),
        flops=1 << 32,
        bytes_accessed=1 << 17,
    )(
        visible.reshape(pixels, visible_num).T,
        jnp.transpose(bins.reshape(pixels, visible_num, samples), (1, 2, 0)),
        ray_code.reshape(pixels, RC),
        blend.reshape(pixels, visible_num).T,
        blank,
    )
    messages = exchange(message, "block", sources)
    table = jnp.asarray(depth_table(samples))

    def serve(own, parts, aside, weights):
        count = len(parts)
        slots = -(-count * capacity // 16) * 16
        slots_all = local_blocks * slots
        outs = [jax.ShapeDtypeStruct((3 * count + 3 * (not own), pixels), F32)]
        if own:
            outs.append(jax.ShapeDtypeStruct((local_blocks, 2 * RC, hidden), BF16))
            outs.append(jax.ShapeDtypeStruct((local_blocks, hidden, 128), BF16))
        return call(
            functools.partial(
                serve_kernel, own, count, slots, tiles_for(count * capacity, list(range(8, slots, 8)))
            ),
            outs,
            [near] * (count + 6 + (not own)),
            ([] if own else [pltpu.VMEM((count * pixels, 2 * RC), BF16)])
            + [
                pltpu.VMEM((slots_all, count * pixels), BF16),
                pltpu.VMEM((slots_all, RC), BF16),
                pltpu.VMEM((slots_all, samples * DC), BF16),
                pltpu.VMEM((-(-slots_all // 128) * 128, 128), F32),
            ],
            flops=2 * slots_all * samples * hidden * (in_width + hidden + 4),
            bytes_accessed=2 * (w_in.size + w_hid.size),
            limit=40 * 1024 * 1024,
        )(*parts, aside, *weights, table, before, *([] if own else [spread]))

    share, first_w, last_w = serve(True, messages[:1], truth, (w_in, w_hid, w_out))
    (partial,) = serve(False, messages[1:], share, (first_w, w_hid, last_w))
    partials = exchange(partial, "block", sources)
    edge, errors = call(
        functools.partial(gather_kernel, sources),
        (
            jax.ShapeDtypeStruct((4, pixels), F32),
            jax.ShapeDtypeStruct((3, pixels), F32),
        ),
        [near] * sources,
        (),
    )(*partials)
    edges = exchange(edge, ("rep", "tile"), columns)
    rendered, flip_map, psnr = call(
        functools.partial(finish_kernel, columns, 3 * sources * columns * pixels),
        (
            jax.ShapeDtypeStruct((3, 1, pixels), F32),
            jax.ShapeDtypeStruct((1, pixels), F32),
            jax.ShapeDtypeStruct((1, 1), F32),
        ),
        [near] * (columns + 2),
        (),
    )(*edges, errors, truth)
    return (rendered, flip_map, psnr.reshape(1))


def solution(mesh):
    placed = (
        P(("groups", "block"), ("rep", "tile"), None),
        P(("groups", "block"), ("rep", "tile"), None, None),
        P(("groups", "block"), ("rep", "tile"), None),
        P(("groups", "block"), ("rep", "tile"), None),
        P(None, ("groups", "block"), ("rep", "tile")),
        P("block", None, None),
        P("block", None, None),
        P("block", None, None),
    )
    return jax.shard_map(
        body,
        mesh=mesh,
        in_specs=placed,
        out_specs=(
            P(None, ("groups", "block"), ("rep", "tile")),
            P(("groups", "block"), ("rep", "tile")),
            P("groups"),
        ),
        check_vma=False,
    )
```

```python
import functools
import math

import jax
import jax.numpy as jnp
import ml_dtypes
import numpy as np
from jax import lax
from jax.experimental import pallas as pl
from jax.experimental.pallas import tpu as pltpu
from jax.sharding import PartitionSpec as P

RC = 128
DC = 16
NBINS = 256
EXTRA = 16
LISTS = 64

OPPONENT = ((0.2126, 0.7152, 0.0722), (0.5, -0.5, 0.0), (0.0, 0.4, -0.4))
SPREAD = (0.6, 0.35, 0.35)
EMPHASIS = (1.0, 2.0, 2.0)

F32 = jnp.float32
BF16 = jnp.bfloat16


def iota(shape, dim):
    return lax.broadcasted_iota(jnp.int32, shape, dim)


def parts_of(values):
    high = values.astype(BF16).astype(F32)
    rest = values - high
    middle = rest.astype(BF16).astype(F32)
    return [high, middle, rest - middle]


def depth_table(sample_num):
    powers = np.arange(DC // 2, dtype=np.float32)
    steps = (np.float32(np.pi) * np.exp2(powers) / np.float32(NBINS)).astype(np.float32)
    angles = np.arange(NBINS, dtype=np.float32)[:, None] * steps
    wide = angles.astype(np.float64)
    code = np.concatenate([np.sin(wide), np.cos(wide)], axis=1).astype(np.float32)
    stride = NBINS // sample_num
    table = np.zeros((NBINS, sample_num, DC), np.float32)
    for row in range(NBINS):
        table[row, row // stride] = code[row]
    return table.reshape(NBINS, sample_num * DC).astype(ml_dtypes.bfloat16)


def layout_kernel(samples, before, spread, blank):
    before[...] = (iota(before.shape, 0) < iota(before.shape, 1)).astype(F32).astype(BF16)
    row = iota(spread.shape[1:], 0)
    here = row % samples == iota(spread.shape[1:], 1) // DC
    for k in range(spread.shape[0]):
        mine = here & (row % LISTS // samples == k)
        spread[k] = mine.astype(F32).astype(BF16)
    blank[...] = jnp.zeros_like(blank)


def pack_kernel(visible, bins, ray_code, blend, blank, message):
    pixels = ray_code.shape[0]
    listed = bins.shape[0] * bins.shape[1]
    message[0:pixels] = ray_code[...]
    message[pixels : pixels + listed] = bins[...].astype(F32).reshape(listed, pixels).astype(BF16)
    shares = blend[...] / jnp.sum(blend[...], axis=0, keepdims=True)
    rows = [visible[...].astype(F32)] + parts_of(shares) + [blank[...]]
    message[pixels + listed :] = jnp.concatenate(rows, axis=0).astype(BF16)


def tiles_for(most, sizes):
    bounds = [0] + [size for size in sizes if size < most] + [-(-most // 8) * 8]
    return [(high, low, high) for low, high in zip(bounds, bounds[1:])]


def lay_out_weights(samples, w_in, w_out, first_w, last_w):
    local_blocks, in_width, hidden = w_in.shape
    for k in range(local_blocks):
        first_w[k, 0:RC] = w_in[k, 0:RC]
        for i in range(RC // DC):
            first_w[k, RC + i * DC : RC + (i + 1) * DC] = w_in[k, RC:]
        wide = jnp.concatenate(
            [
                jnp.broadcast_to(w_out[k, c : c + 1].astype(F32), (samples, hidden))
                for c in range(4)
            ]
            ,
            axis=0,
        )
        rest = jnp.zeros((hidden, 128 - 4 * samples), F32)
        last_w[k] = jnp.concatenate([wide.T, rest], axis=1).astype(BF16)


def serve_kernel(own, sources, slots, tiles, *refs):
    messages = refs[:sources]
    if own:
        aside, w_in, w_hid, w_out, table, before, partial, first_w, last_w = refs[
            sources : sources + 9
        ]
    else:
        aside, first_w, w_hid, last_w, table, before, spread, partial, mixed = refs[
            sources : sources + 9
        ]
    places, codes, depths, heads = refs[-4:]
    local_blocks = w_hid.shape[0]
    pixels = messages[0].shape[1]
    lists = messages[0].shape[0] - pixels - EXTRA
    samples = lists // 2
    if own:
        lay_out_weights(samples, w_in, w_out, first_w, last_w)
    first_block = lax.axis_index("block") * local_blocks

    extras = [messages[s][pixels + lists :].astype(F32) for s in range(sources)]

    named = []
    for s in range(sources):
        block = iota((8, pixels), 0)
        known = (block + first_block).astype(F32)
        named.append(
            [
                ((extras[s][v : v + 1] == known) & (block < local_blocks)).astype(F32)
                for v in range(2)
            ]
        )
    either = [first + second for first, second in named]
    ranks = jnp.dot(
        jnp.concatenate(either, axis=0).astype(BF16), before[...], preferred_element_type=F32
    )
    offset = jnp.zeros((8, 1), F32)
    slot_row = iota((slots, pixels), 0).astype(F32)
    for s in range(sources):
        spot = jnp.where(either[s] > 0.0, ranks[8 * s : 8 * s + 8] + offset, -1.0)
        offset = offset + jnp.sum(either[s], axis=1, keepdims=True)
        for k in range(local_blocks):
            places[k * slots : (k + 1) * slots, s * pixels : (s + 1) * pixels] = (
                (slot_row == spot[k : k + 1]).astype(F32).astype(BF16)
            )
    counts = [jnp.max(offset[k : k + 1]).astype(jnp.int32) for k in range(local_blocks)]

    if own:
        spans = [messages[s][0:pixels] for s in range(sources)]
        codes[...] = jnp.dot(
            places[...], jnp.concatenate(spans, axis=0), preferred_element_type=F32
        ).astype(BF16)
        marks_shape = (samples, DC, pixels)
        mark = (iota(marks_shape, 0) * DC + iota(marks_shape, 1)).astype(F32)
        listed = [messages[s][pixels : pixels + lists].astype(F32) for s in range(sources)]
        for k in range(local_blocks):
            marked = []
            for s in range(sources):
                bins = jnp.where(
                    named[s][0][k : k + 1] > 0.0, listed[s][:samples], listed[s][samples:]
                )
                hit = jnp.broadcast_to(bins[:, None, :], marks_shape) == mark
                marked.append(hit.astype(F32).reshape(samples * DC, pixels).astype(BF16))
            rows = slice(k * slots, (k + 1) * slots)
            is_bin = lax.dot_general(
                places[rows],
                jnp.concatenate(marked, axis=1),
                (((1,), (1,)), ((), ())),
                preferred_element_type=F32,
            ).astype(BF16)
            depths[rows] = jnp.dot(is_bin, table[...], preferred_element_type=F32).astype(BF16)
    else:
        lane = iota((pixels, pixels), 1)
        per_turn = pixels // LISTS
        for turn in range(0, sources, per_turn):
            group = []
            for s in range(turn, min(turn + per_turn, sources)):
                bins = messages[s][pixels : pixels + lists].astype(F32)
                for k in range(local_blocks):
                    group.append(
                        jnp.where(named[s][0][k : k + 1] > 0.0, bins[:samples], bins[samples:])
                    )
                group.append(jnp.zeros((LISTS - local_blocks * samples, pixels), F32))
            rows = sum(part.shape[0] for part in group)
            if rows < pixels:
                group.append(jnp.zeros((pixels - rows, pixels), F32))
            turned = jnp.concatenate(group, axis=0).T
            for s in range(turn, min(turn + per_turn, sources)):
                mixed[s * pixels : (s + 1) * pixels, 0:RC] = messages[s][0:pixels]
                mixed[s * pixels : (s + 1) * pixels, RC:] = jnp.where(
                    lane // LISTS == s - turn, turned, 0.0
                ).astype(BF16)

        chosen = jnp.dot(places[...], mixed[...], preferred_element_type=F32).astype(BF16)
        codes[...] = chosen[:, :RC]
        bins = jnp.concatenate(
            [
                jnp.dot(
                    chosen[k * slots : (k + 1) * slots, RC:], spread[k], preferred_element_type=F32
                )
                for k in range(local_blocks)
            ],
            axis=0,
        )
        is_bin = (bins == iota(bins.shape, 1).astype(F32)).astype(F32).astype(BF16)
        depths[...] = jnp.dot(is_bin, table[...], preferred_element_type=F32).astype(BF16)

    heads[...] = jnp.zeros_like(heads)
    per_half = RC // DC
    def one_block(k, carry):
        count = carry[0]
        for i in range(1, local_blocks):
            count = jnp.where(k == i, carry[i], count)

        def one_tile(start, size):
            rows = pl.ds(pl.multiple_of(k * slots + start, 16), -(-size // 16) * 16)
            code = codes[rows, :]
            depth = depths[rows, :]
            if size % 16:
                code = code.astype(F32)[:size]
                depth = depth.astype(F32)[:size]
            half_lane = iota((size, RC), 1) // DC
            inputs = []
            for j in range(samples):
                half = depth[:, (j // per_half) * RC : (j // per_half + 1) * RC]
                kept = jnp.where(half_lane == j % per_half, half, jnp.zeros_like(half))
                inputs.append(jnp.concatenate([code, kept], axis=1))
            inputs = jnp.concatenate(inputs, axis=0).astype(BF16)
            one = jnp.dot(inputs, first_w[k], preferred_element_type=F32)
            one = jnp.maximum(one, 0.0).astype(BF16)
            two = jnp.dot(one, w_hid[k], preferred_element_type=F32)
            two = jnp.maximum(two, 0.0).astype(BF16)
            out = jnp.dot(two, last_w[k], preferred_element_type=F32)
            sample_lane = iota((size, 128), 1) % samples
            total = jnp.zeros((size, 128), F32)
            for j in range(samples):
                total = jnp.where(sample_lane == j, out[j * size : (j + 1) * size], total)
            heads[pl.ds(pl.multiple_of(k * slots + start, 16), size), :] = total

        def pick(choices):
            if len(choices) == 1:
                one_tile(0, choices[0][0])
                return
            half = len(choices) // 2
            bound = choices[half - 1][2]

            @pl.when(count <= bound)
            def _():
                pick(choices[:half])

            @pl.when(count > bound)
            def _():
                pick(choices[half:])

        @pl.when(count > 0)
        def _():
            pick(tiles)

        return carry

    lax.fori_loop(0, local_blocks, one_block, tuple(counts))

    turned = heads[...].T
    optical = jax.nn.softplus(turned[0:samples]) * (1.5 / samples)
    sample_row = iota(optical.shape, 0)
    ahead = jnp.where(sample_row >= 1, pltpu.roll(optical, 1, 0), 0.0)
    step = 1
    while step < samples:
        ahead = ahead + jnp.where(sample_row >= step, pltpu.roll(ahead, step, 0), 0.0)
        step = 2 * step
    weights = jnp.exp(-ahead) * (1.0 - jnp.exp(-optical))
    background = 1.0 - jnp.sum(weights, axis=0, keepdims=True)
    shades = []
    for c in range(1, 4):
        color = jax.nn.sigmoid(turned[c * samples : (c + 1) * samples])
        shades.append(jnp.sum(weights * color, axis=0, keepdims=True) + background)
    shades.append(jnp.zeros_like(background))
    shades = jnp.concatenate(shades, axis=0)[:, : local_blocks * slots]
    stacked = jnp.concatenate(parts_of(shades) + [jnp.zeros_like(shades)], axis=0).astype(BF16)
    sums = [jnp.zeros((3, pixels), F32)] * sources
    for k in range(local_blocks):
        spots = jnp.dot(
            stacked[:, k * slots : (k + 1) * slots],
            places[k * slots : (k + 1) * slots],
            preferred_element_type=F32,
        )
        spots = spots[0:4] + spots[4:8] + spots[8:12]
        for s in range(sources):
            share = jnp.zeros((1, pixels), F32)
            for v in range(2):
                part = extras[s][2 + v : 3 + v] + extras[s][4 + v : 5 + v] + extras[s][6 + v : 7 + v]
                share = share + named[s][v][k : k + 1] * part
            sums[s] = sums[s] + spots[0:3, s * pixels : (s + 1) * pixels] * share
    if own:
        partial[...] = sums[0] - aside[...].reshape(3, pixels)
    else:
        partial[...] = jnp.concatenate([aside[...]] + sums, axis=0)


def gather_kernel(sources, *refs):
    partials = refs[:sources]
    (message,) = refs[sources:]
    pixels = message.shape[1]
    z = lax.axis_index("block")
    squared = jnp.zeros((3, pixels), F32)
    rows = []
    for u in range(sources):
        difference = partials[0][3 * u : 3 * u + 3]
        for t in range(1, sources):
            difference = difference + partials[t][3 * (t ^ u) : 3 * (t ^ u) + 3]
        squared = squared + difference * difference
        rows.append(difference)
    above = jnp.zeros((3, pixels), F32)
    below = jnp.zeros((3, pixels), F32)
    for u in range(1, sources):
        above = above + jnp.where((z ^ u) == z - 1, rows[u], 0.0)
        below = below + jnp.where((z ^ u) == z + 1, rows[u], 0.0)

    def opponent(block, c):
        return sum(OPPONENT[c][i] * block[i : i + 1] for i in range(3) if OPPONENT[c][i])

    mixed = [
        SPREAD[c] * opponent(above, c) + opponent(rows[0], c) + SPREAD[c] * opponent(below, c)
        for c in range(3)
    ]
    total = jnp.sum(jnp.sum(squared, axis=0, keepdims=True), axis=1, keepdims=True)
    message[...] = jnp.concatenate(
        mixed + [jnp.broadcast_to(total, (1, pixels)), rows[0]], axis=0
    )


def finish_kernel(columns, count, *refs):
    messages = refs[:columns]
    truth, rendered, flip_map, psnr = refs[columns:]
    pixels = flip_map.shape[1]
    q = lax.axis_index("rep") * lax.axis_size("tile") + lax.axis_index("tile")
    rendered[...] = messages[0][4:7].reshape(3, 1, pixels) + truth[...]
    own = messages[0][0:4]
    left = jnp.zeros_like(own)
    right = jnp.zeros_like(own)
    total = own[3:4]
    for s in range(1, columns):
        other = messages[s][0:4]
        left = left + jnp.where((q ^ s) == q - 1, other, 0.0)
        right = right + jnp.where((q ^ s) == q + 1, other, 0.0)
        total = total + other[3:4]
    lane = iota(own.shape, 1)
    before = pltpu.roll(jnp.where(lane == pixels - 1, left, own), 1, 1)
    after = pltpu.roll(jnp.where(lane == 0, right, own), pixels - 1, 1)
    summed = jnp.zeros((1, pixels), F32)
    for c in range(3):
        column = SPREAD[c] * before[c : c + 1] + own[c : c + 1] + SPREAD[c] * after[c : c + 1]
        scale = np.float32(1.0) + np.float32(2.0) * np.float32(SPREAD[c])
        emphasised = EMPHASIS[c] * (column / float(scale * scale))
        summed = summed + emphasised * emphasised
    flip_map[...] = jnp.sqrt(summed + 1e-06)
    logged = jnp.log(total / count + 1e-06) * (-10.0 / math.log(10.0))
    psnr[...] = logged[:, 0:1]


def exchange(value, axes, size):
    out = [value]
    for s in range(1, size):
        out.append(lax.ppermute(value, axes, [(i, i ^ s) for i in range(size)]))
    return out


def call(
    kernel, out_shape, in_specs, scratch, flops=0, bytes_accessed=0, limit=8 << 20
):
    cost = None
    if flops:
        cost = pl.CostEstimate(flops=flops, bytes_accessed=bytes_accessed, transcendentals=0)
    return pl.pallas_call(
        kernel,
        out_shape=out_shape,
        in_specs=in_specs,
        scratch_shapes=list(scratch),
        cost_estimate=cost,
        compiler_params=pltpu.CompilerParams(vmem_limit_bytes=limit),
    )


def body(visible, bins, ray_code, blend, truth, w_in, w_hid, w_out):
    sources = lax.axis_size("block")
    columns = lax.axis_size("rep") * lax.axis_size("tile")
    local_blocks, in_width, hidden = w_in.shape
    pixels = visible.shape[1]
    visible_num = visible.shape[2]
    samples = bins.shape[3]
    blocks_all = local_blocks * sources
    capacity = (2 * pixels * visible_num + blocks_all - 1) // blocks_all
    lists = visible_num * samples
    height = pixels + lists + EXTRA
    far = pl.BlockSpec(memory_space=pltpu.HBM)
    near = pl.BlockSpec(memory_space=pltpu.VMEM)
    before, spread, blank = call(
        functools.partial(layout_kernel, samples),
        (
            jax.ShapeDtypeStruct((pixels, pixels), BF16),
            jax.ShapeDtypeStruct((local_blocks, pixels, samples * DC), BF16),
            jax.ShapeDtypeStruct((EXTRA - 4 * visible_num, pixels), F32),
        ),
        [],
        (),
        flops=1 << 32,
        bytes_accessed=1 << 17,
    )()
    message = call(
        pack_kernel,
        jax.ShapeDtypeStruct((height, pixels), BF16),
        [near] * 5,
        (),
        flops=1 << 32,
        bytes_accessed=1 << 17,
    )(
        visible.reshape(pixels, visible_num).T,
        jnp.transpose(bins.reshape(pixels, visible_num, samples), (1, 2, 0)),
        ray_code.reshape(pixels, RC),
        blend.reshape(pixels, visible_num).T,
        blank,
    )
    messages = exchange(message, "block", sources)
    table = jnp.asarray(depth_table(samples))

    def serve(own, parts, aside, weights):
        count = len(parts)
        slots = -(-count * capacity // 16) * 16
        slots_all = local_blocks * slots
        outs = [jax.ShapeDtypeStruct((3 * count + 3 * (not own), pixels), F32)]
        if own:
            outs.append(jax.ShapeDtypeStruct((local_blocks, 2 * RC, hidden), BF16))
            outs.append(jax.ShapeDtypeStruct((local_blocks, hidden, 128), BF16))
        return call(
            functools.partial(
                serve_kernel, own, count, slots, tiles_for(count * capacity, list(range(8, slots, 8)))
            ),
            outs,
            [near] * (count + 6 + (not own)),
            ([] if own else [pltpu.VMEM((count * pixels, 2 * RC), BF16)])
            + [
                pltpu.VMEM((slots_all, count * pixels), BF16),
                pltpu.VMEM((slots_all, RC), BF16),
                pltpu.VMEM((slots_all, samples * DC), BF16),
                pltpu.VMEM((-(-slots_all // 128) * 128, 128), F32),
            ],
            flops=2 * slots_all * samples * hidden * (in_width + hidden + 4),
            bytes_accessed=2 * (w_in.size + w_hid.size),
            limit=40 * 1024 * 1024,
        )(*parts, aside, *weights, table, before, *([] if own else [spread]))

    share, first_w, last_w = serve(True, messages[:1], truth, (w_in, w_hid, w_out))
    (partial,) = serve(False, messages[1:], share, (first_w, w_hid, last_w))
    partials = exchange(partial, "block", sources)
    edge = call(
        functools.partial(gather_kernel, sources),
        jax.ShapeDtypeStruct((7, pixels), F32),
        [near] * sources,
        (),
    )(*partials)
    edges = exchange(edge, ("rep", "tile"), columns)
    rendered, flip_map, psnr = call(
        functools.partial(finish_kernel, columns, 3 * sources * columns * pixels),
        (
            jax.ShapeDtypeStruct((3, 1, pixels), F32),
            jax.ShapeDtypeStruct((1, pixels), F32),
            jax.ShapeDtypeStruct((1, 1), F32),
        ),
        [near] * (columns + 1),
        (),
    )(*edges, truth)
    return (rendered, flip_map, psnr.reshape(1))


def solution(mesh):
    placed = (
        P(("groups", "block"), ("rep", "tile"), None),
        P(("groups", "block"), ("rep", "tile"), None, None),
        P(("groups", "block"), ("rep", "tile"), None),
        P(("groups", "block"), ("rep", "tile"), None),
        P(None, ("groups", "block"), ("rep", "tile")),
        P("block", None, None),
        P("block", None, None),
        P("block", None, None),
    )
    return jax.shard_map(
        body,
        mesh=mesh,
        in_specs=placed,
        out_specs=(
            P(None, ("groups", "block"), ("rep", "tile")),
            P(("groups", "block"), ("rep", "tile")),
            P("groups"),
        ),
        check_vma=False,
    )
```
